512 devices in a mesh: chan: 128 (over y, z, x_hi), pair: 4 (over x_lo, core).
Axes of the slice: x: 4 (x_hi: 2, x_lo: 2; x = x_hi * 2 + x_lo), y: 4, z: 16, core: 2. Of those that a mesh axis runs over, the one named last changes fastest.
Arguments:
- voltages: bfloat16 [4, 256, 2, 34560], P('pair', 'chan'), may hold values from -6 to 6
- fir_taps: float32 [8, 256], replicated, may hold values from -2 to 2
Outputs:
- visibilities: float32 [128, 2, 1024, 1024], P('chan', None, 'pair')
The draws below stay inside these ranges and needn't reach their ends.
All inputs are finite; a program needn't handle non-finite values.
Results may differ from the reference program's by a relative error of at most 0.0036.
Values may be sent and summed in bfloat16 or wider, within the bound.
A program may use at most 64 MiB of HBM per device.

```python
import math
import jax
import jax.numpy as jnp
from jax import lax

C = 128
P_SIZE = 8
S = 128
NB = 2
A = 1024
N_PAIR = 4


def block_levels(rng, shape, split, low, largest):
    factor_of, own = 1.0, jax.random.fold_in(rng, 6)
    for position, blocks in split:
        heights = jnp.exp(jax.random.uniform(jax.random.fold_in(own, position), (blocks,), jnp.float32, low / len(split), largest / len(split)))
        factor_of = factor_of * jnp.repeat(heights, shape[position] // blocks).reshape([-1 if axis == position else 1 for axis in range(len(shape))])
    return factor_of


def bell_draw(rng, shape, deviation, reach, cuts=(), kind=jnp.bfloat16):
    level = block_levels(rng, shape, cuts, -0.22, 0.18) if cuts else 1.0
    drawn = jax.random.normal(rng, shape, jnp.float32) * deviation * level
    return jnp.minimum(jnp.maximum(drawn, -reach), reach).astype(kind)


def setup_inputs(seed: int = 0) -> dict:
    keys = jax.random.split(jax.random.key(seed), 3)
    return {
        "voltages": bell_draw(keys[0], (N_PAIR, A // N_PAIR, NB, (S + P_SIZE - 1) * 2 * C), 1.0, 6.0, ((0, 4), (1, 128))),
        "fir_taps": bell_draw(keys[1], (P_SIZE, 2 * C), P_SIZE ** -0.5, 2.0, (), jnp.float32),
    }


def dft_rows(channels):
    frame = 2 * channels
    row_index = jnp.arange(2 * channels, dtype=jnp.int32)
    col_index = jnp.arange(frame, dtype=jnp.int32)
    freq_index = row_index // 2
    phases = freq_index[:, None] * col_index[None, :] % frame
    angles = phases.astype(jnp.float32) * (2.0 * math.pi / frame)
    chosen = jnp.where((row_index % 2 == 0)[:, None], jnp.cos(angles), -jnp.sin(angles))
    return chosen * (1.0 / math.sqrt(frame))

def rotate_parts(block_data, spectra_len):
    shaped = block_data.reshape(block_data.shape[:-1] + (block_data.shape[-1] // (2 * spectra_len), 2, spectra_len))
    rotated = jnp.stack([-shaped[..., 1, :], shaped[..., 0, :]], axis=-2)
    return rotated.reshape(block_data.shape)

def reference(voltages, fir_taps):
    frame = 2 * C
    samples = voltages.reshape(A, NB, (S + P_SIZE - 1) * frame)
    transform = dft_rows(C)
    pieces = []
    for batch in range(NB):
        framed = samples[:, batch].astype(jnp.float32).reshape(A, S + P_SIZE - 1, frame)
        filtered = jnp.zeros((A, S, frame), jnp.float32)
        for tap in range(P_SIZE):
            filtered = filtered + fir_taps[tap][None, None, :] * framed[:, tap:tap + S, :]
        spectra = jnp.einsum('wn,asn->aws', transform, filtered, precision=lax.Precision.HIGHEST)
        pieces.append(spectra.reshape(A, C, 2 * S).astype(jnp.bfloat16))
    allspec = jnp.concatenate(pieces, axis=2)
    by_channel = jnp.transpose(allspec, (1, 0, 2))

    def per_channel(block_data):
        as_float = block_data.astype(jnp.float32)
        rotated = rotate_parts(as_float, S)
        real_part = jnp.dot(as_float, as_float.T, precision=lax.Precision.HIGHEST, preferred_element_type=jnp.float32)
        imag_part = jnp.dot(as_float, rotated.T, precision=lax.Precision.HIGHEST, preferred_element_type=jnp.float32)
        return jnp.stack([real_part, imag_part])
    summed = lax.map(per_channel, by_channel)
    return summed * (1.0 / math.sqrt(NB * S))
```

```python
import functools
import math

import jax
import jax.numpy as jnp
import ml_dtypes
import numpy as np
from jax import lax
from jax.experimental import pallas as pl
from jax.experimental.pallas import tpu as pltpu
from jax.sharding import PartitionSpec as P

MESH = pl.DeviceIdType.MESH
NY, NZ, NX = 4, 16, 2
FAR_FIRST = True


def dft_matrix(channels):
    frame = 2 * channels
    part, y, x, z = np.meshgrid(np.arange(2), np.arange(NY), np.arange(NX), np.arange(NZ), indexing="ij")
    freq = ((y * NZ + z) * NX + x).reshape(-1)
    part = part.reshape(-1)
    phases = freq[:, None] * np.arange(frame)[None, :] % frame
    angles = phases * (2.0 * math.pi / frame)
    full = np.where((part == 0)[:, None], np.cos(angles), -np.sin(angles)) / math.sqrt(frame)
    full = full.astype(np.float32)
    high = full.astype(ml_dtypes.bfloat16)
    low = (full - high.astype(np.float32)).astype(ml_dtypes.bfloat16)
    return high, low


def split(value):
    high = value.astype(jnp.bfloat16)
    return high, (value - high.astype(jnp.float32)).astype(jnp.bfloat16)


def nt_dot(a, b):
    return lax.dot_general(a, b, (((1,), (1,)), ((), ())), preferred_element_type=jnp.float32)


def channelize_kernel(volt_ref, taps_ref, high_ref, low_ref, out_ref, wide, filt, inter):
    taps, frame = taps_ref.shape
    half = frame // 2
    frames = volt_ref.shape[0] // 8
    spectra = frames - taps + 1
    wide[...] = volt_ref[...].astype(jnp.float32)
    row = lax.broadcasted_iota(jnp.int32, (8, half), 0)
    second = (row // 2) % 2 == 1
    pattern = []
    for p in range(taps):
        first_half = jnp.broadcast_to(taps_ref[p : p + 1, :half], (8, half))
        other_half = jnp.broadcast_to(taps_ref[p : p + 1, half:], (8, half))
        pattern.append(jnp.where(second, other_half, first_half)[None])
    block = 128
    for j in range(2):
        for part in range(4 * spectra // block):
            base = j * 4 * frames + part * block
            total = None
            for p in range(taps):
                rows = wide[base + 4 * p : base + 4 * p + block, :].reshape(block // 8, 8, half)
                term = rows * pattern[p]
                total = term if total is None else total + term
            at = (j * 4 * spectra) + part * block
            filt[at : at + block, :] = total.reshape(block, half)
    columns = []
    for b in range(2):
        for j in range(2):
            start = j * 4 * spectra + b
            columns.append(
                jnp.concatenate(
                    [
                        filt[pl.ds(start, spectra, stride=4), :],
                        filt[pl.ds(start + 2, spectra, stride=4), :],
                    ],
                    axis=1,
                )
            )
    frames_high, frames_low = split(jnp.concatenate(columns, axis=0))
    high, low = high_ref[...], low_ref[...]
    result = nt_dot(high, frames_high) + (nt_dot(high, frames_low) + nt_dot(low, frames_high))
    channels = high.shape[0] // 2
    for b in range(2):
        for part in range(2):
            for j in range(2):
                at = (b * 2 + part) * 2 * channels + j
                column = (b * 2 + j) * spectra
                inter[pl.ds(at, channels, stride=2), :] = result[
                    part * channels : (part + 1) * channels, column : column + spectra
                ]
    out_ref[...] = inter[...].astype(jnp.bfloat16)


def exchange_kernel(
    src, out, near, local_sem, b_send, b_recv, a_send, a_recv, core_send, core_recv, x_send, x_recv, on_send, on_recv
):
    chan, pair = lax.axis_index("chan"), lax.axis_index("pair")
    y, z, x = chan // (NZ * NX), (chan // NX) % NZ, chan % NX
    core_mate = pair + 1 - 2 * (pair % 2)
    x_mate = (pair + 2) % 4

    def chan_of(y, z, x):
        return (y * NZ + z) * NX + x

    groups = NY * NX
    barrier = pltpu.get_barrier_semaphore()

    def greet(c, p):
        pl.semaphore_signal(barrier, inc=1, device_id={"chan": c, "pair": p}, device_id_type=MESH)

    def other(t):
        d = (y * NX + x + t) % groups
        return d // NX, d % NX

    def step_offset(t):
        t = NZ - 2 - t if FAR_FIRST else t
        m = t // 2 + 1
        return jnp.where(t % 2 == 0, m, NZ - m)

    for t in range(1, groups):
        oy, ox = other(t)
        greet(chan_of(oy, z, ox), pair)
    for t in range(1, NZ):
        greet(chan_of(y, (z + t) % NZ, x), pair)
    greet(chan, core_mate)
    greet(chan, x_mate)
    pl.semaphore_wait(barrier, groups - 1 + NZ - 1 + 2)

    def b_copy(t):
        oy, ox = other(t)
        return pltpu.make_async_remote_copy(
            src_ref=src.at[:, oy, ox],
            dst_ref=near.at[:, y, :, x],
            send_sem=b_send.at[t],
            recv_sem=b_recv.at[t],
            device_id={"chan": chan_of(oy, z, ox), "pair": pair},
            device_id_type=MESH,
        )

    def b_arrival(t):
        d = (y * NX + x - t + groups) % groups
        oy, ox = d // NX, d % NX
        return pltpu.make_async_remote_copy(
            src_ref=src.at[:, oy, ox],
            dst_ref=near.at[:, oy, :, ox],
            send_sem=b_send.at[t],
            recv_sem=b_recv.at[t],
            device_id={"chan": chan_of(oy, z, ox), "pair": pair},
            device_id_type=MESH,
        )

    own = pltpu.make_async_copy(src.at[:, y, x], near.at[:, y, :, x], local_sem.at[0])
    for t in range(1, groups):
        b_copy(t).start()
    own.start()
    own.wait()
    for t in range(1, groups):
        b_arrival(t).wait_recv()

    def a_copy(t):
        oz = (z + step_offset(t)) % NZ
        return pltpu.make_async_remote_copy(
            src_ref=near.at[:, :, oz],
            dst_ref=out.at[:, pair, :, z],
            send_sem=a_send.at[t],
            recv_sem=a_recv.at[t],
            device_id={"chan": chan_of(y, oz, x), "pair": pair},
            device_id_type=MESH,
        )

    def source(t):
        return (z - step_offset(t) + NZ) % NZ

    def a_arrival(t):
        oz = source(t)
        return pltpu.make_async_remote_copy(
            src_ref=near.at[:, :, oz],
            dst_ref=out.at[:, pair, :, oz],
            send_sem=a_send.at[t],
            recv_sem=a_recv.at[t],
            device_id={"chan": chan_of(y, oz, x), "pair": pair},
            device_id_type=MESH,
        )

    def pass_on(block, at, target, send, recv, t):
        return pltpu.make_async_remote_copy(
            src_ref=out.at[:, block, :, at],
            dst_ref=out.at[:, block, :, at],
            send_sem=send.at[t],
            recv_sem=recv.at[t],
            device_id={"chan": chan, "pair": target},
            device_id_type=MESH,
        )

    own_z = pltpu.make_async_copy(near.at[:, :, z], out.at[:, pair, :, z], local_sem.at[1])
    own_z.start()

    @pl.loop(0, NZ - 1)
    def _(t):
        a_copy(t).start()

    own_z.wait()
    pass_on(pair, z, x_mate, x_send, x_recv, NZ - 1).start()
    pass_on(pair, z, core_mate, core_send, core_recv, NZ - 1).start()

    @pl.loop(0, NZ - 1)
    def _(t):
        a_arrival(t).wait_recv()
        pass_on(pair, source(t), x_mate, x_send, x_recv, t).start()
        pass_on(pair, source(t), core_mate, core_send, core_recv, t).start()
        previous = (t + NZ - 1) % NZ
        at = jnp.where(t == 0, z, source(previous))
        pass_on(x_mate, at, x_mate, x_send, x_recv, previous).wait_recv()
        pass_on(x_mate, at, core_mate, on_send, on_recv, previous).start()

    last = NZ - 2
    pass_on(x_mate, source(last), x_mate, x_send, x_recv, last).wait_recv()
    pass_on(x_mate, source(last), core_mate, on_send, on_recv, last).start()

    diagonal = (core_mate + 2) % 4

    @pl.loop(0, NZ)
    def _(t):
        at = jnp.where(t == NZ - 1, z, source(t))
        pass_on(core_mate, at, core_mate, core_send, core_recv, t).wait_recv()
        pass_on(diagonal, at, core_mate, on_send, on_recv, t).wait_recv()
        pass_on(pair, at, core_mate, core_send, core_recv, t).wait_send()
        pass_on(pair, at, x_mate, x_send, x_recv, t).wait_send()
        pass_on(x_mate, at, core_mate, on_send, on_recv, t).wait_send()

    @pl.loop(0, NZ - 1)
    def _(t):
        a_copy(t).wait_send()

    for t in range(1, groups):
        b_copy(t).wait_send()


def correlate_kernel(scale, rows_ref, own_ref, out_ref):
    wide = [rows_ref[q] for q in range(4)]
    own = [own_ref[q] for q in range(4)]
    columns = jnp.concatenate(wide, axis=1)
    straight = jnp.concatenate(own, axis=1)
    turned = jnp.concatenate([own[1], -own[0], own[3], -own[2]], axis=1)
    out_ref[0] = nt_dot(straight, columns) * scale
    out_ref[1] = nt_dot(turned, columns) * scale


def shards(voltages, fir_taps):
    _, antennas, batches, samples = voltages.shape
    taps, frame = fir_taps.shape
    frames = samples // frame
    spectra_len = frames - taps + 1
    half = frame // 2
    volt = voltages.reshape(antennas, batches, samples // half, half)
    volt = jnp.transpose(volt, (0, 2, 1, 3)).reshape(antennas * batches * samples // half, half)
    high, low = dft_matrix(half)
    vmem = pl.BlockSpec(memory_space=pltpu.VMEM)
    spectra = pl.pallas_call(
        channelize_kernel,
        out_shape=jax.ShapeDtypeStruct((8 * half, spectra_len), jnp.bfloat16),
        in_specs=[vmem] * 4,
        out_specs=vmem,
        scratch_shapes=[
            pltpu.VMEM(volt.shape, jnp.float32),
            pltpu.VMEM((8 * spectra_len, half), jnp.float32),
            pltpu.VMEM((8 * half, spectra_len), jnp.float32),
        ],
        compiler_params=pltpu.CompilerParams(vmem_limit_bytes=16 * 1024 * 1024),
    )(volt, fir_taps, jnp.asarray(high), jnp.asarray(low))
    spectra = spectra.reshape(4, NY, NX, NZ, 2, spectra_len)
    dma = pltpu.SemaphoreType.DMA
    everyone = pl.pallas_call(
        exchange_kernel,
        out_shape=jax.ShapeDtypeStruct((4, 4, NY, NZ, NX, 2, spectra_len), jnp.bfloat16),
        in_specs=[pl.BlockSpec(memory_space=pl.ANY)],
        out_specs=pl.BlockSpec(memory_space=pl.ANY),
        scratch_shapes=[
            pltpu.VMEM((4, NY, NZ, NX, 2, spectra_len), jnp.bfloat16),
            dma((2,)),
            dma((NY * NX,)),
            dma((NY * NX,)),
        ]
        + [dma((NZ,))] * 8,
        compiler_params=pltpu.CompilerParams(
            collective_id=0, has_side_effects=True, vmem_limit_bytes=16 * 1024 * 1024
        ),
    )(spectra)
    everyone = everyone.reshape(4, 4 * NY * NZ * NX * 2, spectra_len)
    total = everyone.shape[1]
    block = total // 4
    tile = 256
    index = lax.axis_index("pair")
    scale = 1.0 / math.sqrt(batches * spectra_len)
    own_rows = lax.dynamic_slice_in_dim(everyone, index * block, block, axis=1)
    return pl.pallas_call(
        functools.partial(correlate_kernel, scale),
        grid=(total // tile,),
        out_shape=jax.ShapeDtypeStruct((1, 2, block, total), jnp.float32),
        in_specs=[
            pl.BlockSpec((4, tile, spectra_len), lambda g: (0, g, 0)),
            pl.BlockSpec((4, block, spectra_len), lambda g: (0, 0, 0)),
        ],
        out_specs=pl.BlockSpec((None, 2, block, tile), lambda g: (0, 0, 0, g)),
        compiler_params=pltpu.CompilerParams(vmem_limit_bytes=16 * 1024 * 1024),
    )(everyone, own_rows)


def solution(mesh):
    in_specs = (P("pair", "chan", None, None), P())
    out_specs = P("chan", None, "pair", None)
    return jax.shard_map(shards, mesh=mesh, in_specs=in_specs, out_specs=out_specs, check_vma=False)
```

```python
import functools
import math

import jax
import jax.numpy as jnp
import ml_dtypes
import numpy as np
from jax import lax
from jax.experimental import pallas as pl
from jax.experimental.layout import Layout, with_layout_constraint
from jax.experimental.pallas import tpu as pltpu
from jax.sharding import PartitionSpec as P

MESH = pl.DeviceIdType.MESH
NY, NZ, NX = 4, 16, 2
QUADS = NZ // 4
GROUPS = NY * NX
VMEM_LIMIT = 56 * 1024 * 1024
Z_STEPS = (
    [(2, k) for k in range(4)]
    + [(r, k) for k in range(4) for r in (1, 3)]
    + [(0, k) for k in range(1, 4)]
)
QUAD_ORDER = (2, 1, 3, 0)


def dft_matrix(channels):
    frame = 2 * channels
    part, y, x, z = np.meshgrid(np.arange(2), np.arange(NY), np.arange(NX), np.arange(NZ), indexing="ij")
    freq = ((y * NZ + z) * NX + x).reshape(-1)
    part = part.reshape(-1)
    phases = freq[:, None] * np.arange(frame)[None, :] % frame
    angles = phases * (2.0 * math.pi / frame)
    full = np.where((part == 0)[:, None], np.cos(angles), -np.sin(angles)) / math.sqrt(frame)
    full = full.astype(np.float32)
    high = full.astype(ml_dtypes.bfloat16)
    low = (full - high.astype(np.float32)).astype(ml_dtypes.bfloat16)
    return high, low


def split(value):
    high = value.astype(jnp.bfloat16)
    return high, (value - high.astype(jnp.float32)).astype(jnp.bfloat16)


def nt_dot(a, b):
    return lax.dot_general(a, b, (((1,), (1,)), ((), ())), preferred_element_type=jnp.float32)


def channelize(volt, taps_ref, high_ref, low_ref, spec, wide, filt, inter):
    taps, frame = taps_ref.shape
    half = frame // 2
    frames = volt.shape[0] // 8
    spectra = frames - taps + 1
    wide[...] = volt[...].astype(jnp.float32)
    row = lax.broadcasted_iota(jnp.int32, (8, half), 0)
    second = (row // 2) % 2 == 1
    pattern = []
    for p in range(taps):
        first_half = jnp.broadcast_to(taps_ref[p : p + 1, :half], (8, half))
        other_half = jnp.broadcast_to(taps_ref[p : p + 1, half:], (8, half))
        pattern.append(jnp.where(second, other_half, first_half)[None])
    block = 128
    for j in range(2):
        for part in range(4 * spectra // block):
            base = j * 4 * frames + part * block
            total = None
            for p in range(taps):
                rows = wide[base + 4 * p : base + 4 * p + block, :].reshape(block // 8, 8, half)
                term = rows * pattern[p]
                total = term if total is None else total + term
            at = (j * 4 * spectra) + part * block
            filt[at : at + block, :] = total.reshape(block, half)
    columns = []
    for b in range(2):
        for j in range(2):
            start = j * 4 * spectra + b
            columns.append(
                jnp.concatenate(
                    [
                        filt[pl.ds(start, spectra, stride=4), :],
                        filt[pl.ds(start + 2, spectra, stride=4), :],
                    ],
                    axis=1,
                )
            )
    frames_high, frames_low = split(jnp.concatenate(columns, axis=0))
    high, low = high_ref[...], low_ref[...]
    result = nt_dot(high, frames_high) + (nt_dot(high, frames_low) + nt_dot(low, frames_high))
    channels = high.shape[0] // 2
    for b in range(2):
        for part in range(2):
            for j in range(2):
                column = (b * 2 + j) * spectra
                inter[b, part, :, j, :] = result[
                    part * channels : (part + 1) * channels, column : column + spectra
                ]
    for b in range(2):
        for part in range(2):
            spec[b, part] = (
                inter[b, part].astype(jnp.bfloat16).reshape(NY, NX, NZ, 2, spectra)
            )


def spread_kernel(
    volt_hbm, taps_hbm, high_hbm, low_hbm, out,
    volt, taps, high, low, wide, filt, inter, spec, near,
    load_sem, own_sem, b_send, b_recv, a_send, a_recv, core_send, core_recv, x_send, x_recv, on_send, on_recv,
):
    loads = [
        pltpu.make_async_copy(source, target, load_sem.at[i])
        for i, (source, target) in enumerate(((volt_hbm, volt), (taps_hbm, taps), (high_hbm, high), (low_hbm, low)))
    ]
    for load in loads:
        load.start()

    chan, pair = lax.axis_index("chan"), lax.axis_index("pair")
    y, z, x = chan // (NZ * NX), (chan // NX) % NZ, chan % NX
    quad, place = z // 4, z % 4
    core_mate = pair + 1 - 2 * (pair % 2)
    x_mate = (pair + 2) % 4

    def chan_of(y, z, x):
        return (y * NZ + z) * NX + x

    def group_ahead(t):
        d = (y * NX + x + t) % GROUPS
        return d // NX, d % NX

    def z_ahead(r, k):
        return (quad + r) % QUADS * 4 + (place + k) % 4

    def z_behind(r, k):
        return (quad - r + QUADS) % QUADS * 4 + (place - k + 4) % 4

    barrier = pltpu.get_barrier_semaphore()

    def greet(c, p):
        pl.semaphore_signal(barrier, inc=1, device_id={"chan": c, "pair": p}, device_id_type=MESH)

    for r, k in Z_STEPS:
        greet(chan_of(y, z_ahead(r, k), x), pair)
    for t in range(1, GROUPS):
        oy, ox = group_ahead(t)
        greet(chan_of(oy, z, ox), pair)
    greet(chan, x_mate)
    greet(chan, core_mate)

    for load in loads:
        load.wait()
    channelize(volt, taps, high, low, spec, wide, filt, inter)
    pl.semaphore_wait(barrier, len(Z_STEPS) + GROUPS - 1 + 2)

    def remote(source, target, send, recv, c, p):
        return pltpu.make_async_remote_copy(
            src_ref=source, dst_ref=target, send_sem=send, recv_sem=recv,
            device_id={"chan": c, "pair": p}, device_id_type=MESH,
        )

    def b_copy(b, t):
        oy, ox = group_ahead(t)
        return remote(
            spec.at[b, :, oy, ox], near.at[b, :, y, :, x],
            b_send.at[b, t], b_recv.at[b, t], chan_of(oy, z, ox), pair,
        )

    def b_arrival(b, t):
        oy, ox = group_ahead(GROUPS - t)
        return remote(
            spec.at[b, :, oy, ox], near.at[b, :, oy, :, ox],
            b_send.at[b, t], b_recv.at[b, t], chan_of(oy, z, ox), pair,
        )

    def a_copy(b, r, k):
        oz = z_ahead(r, k)
        return remote(
            near.at[b, :, :, oz], out.at[b, :, pair, :, z],
            a_send.at[b, r * 4 + k], a_recv.at[b, r * 4 + k], chan_of(y, oz, x), pair,
        )

    def a_arrival(b, r, k):
        oz = z_behind(r, k)
        return remote(
            near.at[b, :, :, oz], out.at[b, :, pair, :, oz],
            a_send.at[b, r * 4 + k], a_recv.at[b, r * 4 + k], chan_of(y, oz, x), pair,
        )

    def pass_on(b, block, r, target, send, recv):
        at = pl.ds((quad - r + QUADS) % QUADS * 4, 4)
        ref = out.at[b, :, block, :, at]
        return remote(ref, ref, send.at[b, r], recv.at[b, r], chan, target)

    own = [pltpu.make_async_copy(spec.at[b, :, y, x], near.at[b, :, y, :, x], own_sem.at[b]) for b in range(2)]
    own_z = [pltpu.make_async_copy(near.at[b, :, :, z], out.at[b, :, pair, :, z], own_sem.at[2 + b]) for b in range(2)]

    for b in range(2):
        for t in range(1, GROUPS):
            b_copy(b, t).start()
        own[b].start()
    for b in range(2):
        own[b].wait()
        for t in range(1, GROUPS):
            b_arrival(b, t).wait_recv()
        for r, k in Z_STEPS:
            a_copy(b, r, k).start()
        own_z[b].start()

    def gather(b, r):
        for k in range(4):
            if r or k:
                a_arrival(b, r, k).wait_recv()
        if r == 0:
            own_z[b].wait()
        pass_on(b, pair, r, x_mate, x_send, x_recv).start()
        pass_on(b, pair, r, core_mate, core_send, core_recv).start()

    def forward(b, r):
        pass_on(b, x_mate, r, x_mate, x_send, x_recv).wait_recv()
        pass_on(b, x_mate, r, core_mate, on_send, on_recv).start()

    for r in QUAD_ORDER:
        gather(0, r)
    for r in QUAD_ORDER:
        forward(0, r)
        gather(1, r)
    for r in QUAD_ORDER:
        forward(1, r)

    diagonal = (core_mate + 2) % 4
    for b in range(2):
        for r in range(QUADS):
            pass_on(b, core_mate, r, core_mate, core_send, core_recv).wait_recv()
            pass_on(b, diagonal, r, core_mate, on_send, on_recv).wait_recv()
            pass_on(b, pair, r, core_mate, core_send, core_recv).wait_send()
            pass_on(b, pair, r, x_mate, x_send, x_recv).wait_send()
            pass_on(b, x_mate, r, core_mate, on_send, on_recv).wait_send()
        for r, k in Z_STEPS:
            a_copy(b, r, k).wait_send()
        for t in range(1, GROUPS):
            b_copy(b, t).wait_send()


def correlate_kernel(scale, everyone, out, held, own, result, in_sem, out_sem):
    tiles, _, block, tile = result.shape
    mine = pl.ds(pl.multiple_of(lax.axis_index("pair") * block, block), block)
    own_load = pltpu.make_async_copy(everyone.at[:, mine], own, in_sem.at[tiles])
    own_load.start()
    loads, stores = [], []
    for g in range(tiles):
        there = pl.ds(g * tile, tile)
        loads.append(pltpu.make_async_copy(everyone.at[:, there], held.at[g], in_sem.at[g]))
        stores.append(pltpu.make_async_copy(result.at[g], out.at[0, :, :, there], out_sem.at[g]))
        loads[g].start()
    own_load.wait()
    rows = [own[q] for q in range(4)]
    straight = jnp.concatenate(rows, axis=1)
    turned = jnp.concatenate([rows[1], -rows[0], rows[3], -rows[2]], axis=1)
    for g in range(tiles):
        loads[g].wait()
        columns = jnp.concatenate([held[g, q] for q in range(4)], axis=1)
        result[g, 0] = nt_dot(straight, columns) * scale
        result[g, 1] = nt_dot(turned, columns) * scale
        stores[g].start()
    for store in stores:
        store.wait()


def shards(voltages, fir_taps):
    _, antennas, batches, samples = voltages.shape
    taps, frame = fir_taps.shape
    frames = samples // frame
    spectra_len = frames - taps + 1
    half = frame // 2
    volt = voltages.reshape(antennas, batches, samples // half, half)
    volt = with_layout_constraint(volt, Layout(major_to_minor=(0, 2, 1, 3)))
    volt = jnp.transpose(volt, (0, 2, 1, 3)).reshape(antennas * batches * samples // half, half)
    high, low = dft_matrix(half)
    hbm = pl.BlockSpec(memory_space=pltpu.HBM)
    dma = pltpu.SemaphoreType.DMA
    everyone = pl.pallas_call(
        spread_kernel,
        out_shape=jax.ShapeDtypeStruct((2, 2, 4, NY, NZ, NX, 2, spectra_len), jnp.bfloat16),
        in_specs=[hbm] * 4,
        out_specs=hbm,
        scratch_shapes=[
            pltpu.VMEM(volt.shape, jnp.bfloat16),
            pltpu.VMEM(fir_taps.shape, jnp.float32),
            pltpu.VMEM(high.shape, jnp.bfloat16),
            pltpu.VMEM(low.shape, jnp.bfloat16),
            pltpu.VMEM(volt.shape, jnp.float32),
            pltpu.VMEM((8 * spectra_len, half), jnp.float32),
            pltpu.VMEM((2, 2, half, 2, spectra_len), jnp.float32),
            pltpu.VMEM((2, 2, NY, NX, NZ, 2, spectra_len), jnp.bfloat16),
            pltpu.VMEM((2, 2, NY, NZ, NX, 2, spectra_len), jnp.bfloat16),
            dma((4,)),
            dma((4,)),
            dma((2, GROUPS)),
            dma((2, GROUPS)),
            dma((2, NZ)),
            dma((2, NZ)),
        ]
        + [dma((2, QUADS))] * 6,
        compiler_params=pltpu.CompilerParams(
            collective_id=0, has_side_effects=True, vmem_limit_bytes=VMEM_LIMIT
        ),
    )(volt, fir_taps, jnp.asarray(high), jnp.asarray(low))
    everyone = everyone.reshape(4, 4 * NY * NZ * NX * 2, spectra_len)
    total = everyone.shape[1]
    block = total // 4
    tiles = 4
    tile = total // tiles
    scale = 1.0 / math.sqrt(batches * spectra_len)
    return pl.pallas_call(
        functools.partial(correlate_kernel, scale),
        out_shape=jax.ShapeDtypeStruct((1, 2, block, total), jnp.float32),
        in_specs=[hbm],
        out_specs=hbm,
        scratch_shapes=[
            pltpu.VMEM((tiles, 4, tile, spectra_len), jnp.bfloat16),
            pltpu.VMEM((4, block, spectra_len), jnp.bfloat16),
            pltpu.VMEM((tiles, 2, block, tile), jnp.float32),
            dma((tiles + 1,)),
            dma((tiles,)),
        ],
        compiler_params=pltpu.CompilerParams(vmem_limit_bytes=VMEM_LIMIT),
    )(everyone)


def solution(mesh):
    in_specs = (P("pair", "chan", None, None), P())
    out_specs = P("chan", None, "pair", None)
    return jax.shard_map(shards, mesh=mesh, in_specs=in_specs, out_specs=out_specs, check_vma=False)
```

```python
import functools
import math

import jax
import jax.numpy as jnp
import ml_dtypes
import numpy as np
from jax import lax
from jax.experimental import pallas as pl
from jax.experimental.layout import Layout, with_layout_constraint
from jax.experimental.pallas import tpu as pltpu
from jax.sharding import PartitionSpec as P

MESH = pl.DeviceIdType.MESH
NY, NZ, NX = 4, 16, 2
QUADS = NZ // 4
GROUPS = NY * NX
VMEM_LIMIT = 56 * 1024 * 1024
Z_STEPS = (
    [(2, k) for k in range(4)]
    + [(r, k) for k in range(4) for r in (1, 3)]
    + [(0, k) for k in range(1, 4)]
)


def dft_matrix(channels):
    frame = 2 * channels
    part, y, x, z = np.meshgrid(np.arange(2), np.arange(NY), np.arange(NX), np.arange(NZ), indexing="ij")
    freq = ((y * NZ + z) * NX + x).reshape(-1)
    part = part.reshape(-1)
    phases = freq[:, None] * np.arange(frame)[None, :] % frame
    angles = phases * (2.0 * math.pi / frame)
    full = np.where((part == 0)[:, None], np.cos(angles), -np.sin(angles)) / math.sqrt(frame)
    full = full.astype(np.float32)
    high = full.astype(ml_dtypes.bfloat16)
    low = (full - high.astype(np.float32)).astype(ml_dtypes.bfloat16)
    return high, low


def split(value):
    high = value.astype(jnp.bfloat16)
    return high, (value - high.astype(jnp.float32)).astype(jnp.bfloat16)


def nt_dot(a, b):
    return lax.dot_general(a, b, (((1,), (1,)), ((), ())), preferred_element_type=jnp.float32)


def channelize(volt, taps_ref, high_ref, low_ref, spec, wide, filt, inter):
    taps, frame = taps_ref.shape
    half = frame // 2
    frames = volt.shape[0] // 8
    spectra = frames - taps + 1
    wide[...] = volt[...].astype(jnp.float32)
    row = lax.broadcasted_iota(jnp.int32, (8, half), 0)
    second = (row // 2) % 2 == 1
    pattern = []
    for p in range(taps):
        first_half = jnp.broadcast_to(taps_ref[p : p + 1, :half], (8, half))
        other_half = jnp.broadcast_to(taps_ref[p : p + 1, half:], (8, half))
        pattern.append(jnp.where(second, other_half, first_half)[None])
    block = 128
    for j in range(2):
        for part in range(4 * spectra // block):
            base = j * 4 * frames + part * block
            total = None
            for p in range(taps):
                rows = wide[base + 4 * p : base + 4 * p + block, :].reshape(block // 8, 8, half)
                term = rows * pattern[p]
                total = term if total is None else total + term
            at = (j * 4 * spectra) + part * block
            filt[at : at + block, :] = total.reshape(block, half)
    columns = []
    for b in range(2):
        for j in range(2):
            start = j * 4 * spectra + b
            columns.append(
                jnp.concatenate(
                    [
                        filt[pl.ds(start, spectra, stride=4), :],
                        filt[pl.ds(start + 2, spectra, stride=4), :],
                    ],
                    axis=1,
                )
            )
    frames_high, frames_low = split(jnp.concatenate(columns, axis=0))
    high, low = high_ref[...], low_ref[...]
    result = nt_dot(high, frames_high) + (nt_dot(high, frames_low) + nt_dot(low, frames_high))
    channels = high.shape[0] // 2
    for b in range(2):
        for part in range(2):
            for j in range(2):
                column = (b * 2 + j) * spectra
                inter[b, part, :, j, :] = result[
                    part * channels : (part + 1) * channels, column : column + spectra
                ]
    for b in range(2):
        for part in range(2):
            spec[b * 2 + part] = (
                inter[b, part].astype(jnp.bfloat16).reshape(NY, NX, NZ, 2, spectra)
            )


def spread_kernel(
    volt_hbm, taps_hbm, high_hbm, low_hbm, out,
    volt, taps, high, low, wide, filt, inter, spec, near,
    load_sem, own_sem, b_send, b_recv, a_send, a_recv, core_send, core_recv, x_send, x_recv, on_send, on_recv,
):
    loads = [
        pltpu.make_async_copy(source, target, load_sem.at[i])
        for i, (source, target) in enumerate(((volt_hbm, volt), (taps_hbm, taps), (high_hbm, high), (low_hbm, low)))
    ]
    for load in loads:
        load.start()

    chan, pair = lax.axis_index("chan"), lax.axis_index("pair")
    y, z, x = chan // (NZ * NX), (chan // NX) % NZ, chan % NX
    quad, place = z // 4, z % 4
    core_mate = pair + 1 - 2 * (pair % 2)
    x_mate = (pair + 2) % 4

    def chan_of(y, z, x):
        return (y * NZ + z) * NX + x

    def group_ahead(t):
        d = (y * NX + x + t) % GROUPS
        return d // NX, d % NX

    def z_ahead(r, k):
        return (quad + r) % QUADS * 4 + (place + k) % 4

    def z_behind(r, k):
        return (quad - r + QUADS) % QUADS * 4 + (place - k + 4) % 4

    barrier = pltpu.get_barrier_semaphore()

    def greet(c, p):
        pl.semaphore_signal(barrier, inc=1, device_id={"chan": c, "pair": p}, device_id_type=MESH)

    for r, k in Z_STEPS:
        greet(chan_of(y, z_ahead(r, k), x), pair)
    for t in range(1, GROUPS):
        oy, ox = group_ahead(t)
        greet(chan_of(oy, z, ox), pair)
    greet(chan, x_mate)
    greet(chan, core_mate)

    for load in loads:
        load.wait()
    channelize(volt, taps, high, low, spec, wide, filt, inter)
    pl.semaphore_wait(barrier, len(Z_STEPS) + GROUPS - 1 + 2)

    def remote(source, target, send, recv, c, p):
        return pltpu.make_async_remote_copy(
            src_ref=source, dst_ref=target, send_sem=send, recv_sem=recv,
            device_id={"chan": c, "pair": p}, device_id_type=MESH,
        )

    def b_copy(q, t):
        oy, ox = group_ahead(t)
        return remote(
            spec.at[q, oy, ox], near.at[q, y, :, x], b_send.at[q, t], b_recv.at[q, t], chan_of(oy, z, ox), pair
        )

    def b_arrival(q, t):
        oy, ox = group_ahead(GROUPS - t)
        return remote(
            spec.at[q, oy, ox], near.at[q, oy, :, ox], b_send.at[q, t], b_recv.at[q, t], chan_of(oy, z, ox), pair
        )

    def a_copy(q, r, k):
        oz = z_ahead(r, k)
        return remote(
            near.at[q, :, oz], out.at[q, pair, :, z],
            a_send.at[q, r * 4 + k], a_recv.at[q, r * 4 + k], chan_of(y, oz, x), pair,
        )

    def a_arrival(q, r, k):
        oz = z_behind(r, k)
        return remote(
            near.at[q, :, oz], out.at[q, pair, :, oz],
            a_send.at[q, r * 4 + k], a_recv.at[q, r * 4 + k], chan_of(y, oz, x), pair,
        )

    def pass_on(q, block, target, send, recv):
        ref = out.at[q, block]
        return remote(ref, ref, send.at[q], recv.at[q], chan, target)

    own = [pltpu.make_async_copy(spec.at[q, y, x], near.at[q, y, :, x], own_sem.at[q]) for q in range(4)]
    own_z = [pltpu.make_async_copy(near.at[q, :, z], out.at[q, pair, :, z], own_sem.at[4 + q]) for q in range(4)]

    for q in range(4):
        for t in range(1, GROUPS):
            b_copy(q, t).start()
        own[q].start()
    for q in range(4):
        own[q].wait()
        for t in range(1, GROUPS):
            b_arrival(q, t).wait_recv()
        for r, k in Z_STEPS:
            a_copy(q, r, k).start()
        own_z[q].start()

    def gather(q):
        for r, k in Z_STEPS:
            a_arrival(q, r, k).wait_recv()
        own_z[q].wait()
        pass_on(q, pair, x_mate, x_send, x_recv).start()
        pass_on(q, pair, core_mate, core_send, core_recv).start()

    def forward(q):
        pass_on(q, x_mate, x_mate, x_send, x_recv).wait_recv()
        pass_on(q, x_mate, core_mate, on_send, on_recv).start()

    gather(0)
    for q in range(1, 4):
        gather(q)
        forward(q - 1)
    forward(3)

    diagonal = (core_mate + 2) % 4
    for q in range(4):
        pass_on(q, core_mate, core_mate, core_send, core_recv).wait_recv()
        pass_on(q, diagonal, core_mate, on_send, on_recv).wait_recv()
        pass_on(q, pair, core_mate, core_send, core_recv).wait_send()
        pass_on(q, pair, x_mate, x_send, x_recv).wait_send()
        pass_on(q, x_mate, core_mate, on_send, on_recv).wait_send()
        for r, k in Z_STEPS:
            a_copy(q, r, k).wait_send()
        for t in range(1, GROUPS):
            b_copy(q, t).wait_send()


def correlate_kernel(scale, everyone, out, result, out_sem):
    tiles, _, block, tile = result.shape
    mine = pl.ds(pl.multiple_of(lax.axis_index("pair") * block, block), block)
    rows = [everyone[q, mine, :] for q in range(4)]
    straight = jnp.concatenate(rows, axis=1)
    turned = jnp.concatenate([rows[1], -rows[0], rows[3], -rows[2]], axis=1)
    stores = []
    for g in range(tiles):
        there = pl.ds(g * tile, tile)
        columns = jnp.concatenate([everyone[q, there, :] for q in range(4)], axis=1)
        result[g, 0] = nt_dot(straight, columns) * scale
        result[g, 1] = nt_dot(turned, columns) * scale
        stores.append(pltpu.make_async_copy(result.at[g], out.at[0, :, :, there], out_sem.at[g]))
        stores[g].start()
    for store in stores:
        store.wait()


def shards(voltages, fir_taps):
    _, antennas, batches, samples = voltages.shape
    taps, frame = fir_taps.shape
    frames = samples // frame
    spectra_len = frames - taps + 1
    half = frame // 2
    volt = voltages.reshape(antennas, batches, samples // half, half)
    volt = with_layout_constraint(volt, Layout(major_to_minor=(0, 2, 1, 3)))
    volt = jnp.transpose(volt, (0, 2, 1, 3)).reshape(antennas * batches * samples // half, half)
    high, low = dft_matrix(half)
    hbm = pl.BlockSpec(memory_space=pltpu.HBM)
    vmem = pl.BlockSpec(memory_space=pltpu.VMEM)
    dma = pltpu.SemaphoreType.DMA
    everyone = pl.pallas_call(
        spread_kernel,
        out_shape=pltpu.VMEM((4, 4, NY, NZ, NX, 2, spectra_len), jnp.bfloat16),
        in_specs=[hbm] * 4,
        out_specs=vmem,
        scratch_shapes=[
            pltpu.VMEM(volt.shape, jnp.bfloat16),
            pltpu.VMEM(fir_taps.shape, jnp.float32),
            pltpu.VMEM(high.shape, jnp.bfloat16),
            pltpu.VMEM(low.shape, jnp.bfloat16),
            pltpu.VMEM(volt.shape, jnp.float32),
            pltpu.VMEM((8 * spectra_len, half), jnp.float32),
            pltpu.VMEM((2, 2, half, 2, spectra_len), jnp.float32),
            pltpu.VMEM((4, NY, NX, NZ, 2, spectra_len), jnp.bfloat16),
            pltpu.VMEM((4, NY, NZ, NX, 2, spectra_len), jnp.bfloat16),
            dma((4,)),
            dma((8,)),
            dma((4, GROUPS)),
            dma((4, GROUPS)),
            dma((4, NZ)),
            dma((4, NZ)),
        ]
        + [dma((4,))] * 6,
        compiler_params=pltpu.CompilerParams(
            collective_id=0, has_side_effects=True, vmem_limit_bytes=VMEM_LIMIT
        ),
    )(volt, fir_taps, jnp.asarray(high), jnp.asarray(low))
    everyone = everyone.reshape(4, 4 * NY * NZ * NX * 2, spectra_len)
    total = everyone.shape[1]
    block = total // 4
    tiles = 4
    tile = total // tiles
    scale = 1.0 / math.sqrt(batches * spectra_len)
    return pl.pallas_call(
        functools.partial(correlate_kernel, scale),
        out_shape=jax.ShapeDtypeStruct((1, 2, block, total), jnp.float32),
        in_specs=[vmem],
        out_specs=hbm,
        scratch_shapes=[pltpu.VMEM((tiles, 2, block, tile), jnp.float32), dma((tiles,))],
        compiler_params=pltpu.CompilerParams(vmem_limit_bytes=8 * 1024 * 1024),
    )(everyone)


def solution(mesh):
    in_specs = (P("pair", "chan", None, None), P())
    out_specs = P("chan", None, "pair", None)
    return jax.shard_map(shards, mesh=mesh, in_specs=in_specs, out_specs=out_specs, check_vma=False)
```

```python
import functools
import math

import jax
import jax.numpy as jnp
import ml_dtypes
import numpy as np
from jax import lax
from jax.experimental import pallas as pl
from jax.experimental.layout import Layout, with_layout_constraint
from jax.experimental.pallas import tpu as pltpu
from jax.sharding import PartitionSpec as P

MESH = pl.DeviceIdType.MESH
NY, NZ, NX = 4, 16, 2
QUADS = NZ // 4
PARTS = 2
PLANE_STEPS = sorted(
    ((dy, dx) for dy in range(NY) for dx in range(2 * NX) if dy or dx),
    key=lambda step: -(min(step[0], NY - step[0]) + min(step[1], 2 * NX - step[1])),
)
VMEM_LIMIT = 56 * 1024 * 1024
Z_STEPS = (
    [(2, k) for k in range(4)]
    + [(r, k) for k in range(4) for r in (1, 3)]
    + [(0, k) for k in range(1, 4)]
)


def dft_matrix(channels):
    frame = 2 * channels
    part, z, y, x = np.meshgrid(np.arange(2), np.arange(NZ), np.arange(NY), np.arange(NX), indexing="ij")
    freq = ((y * NZ + z) * NX + x).reshape(-1)
    part = part.reshape(-1)
    phases = freq[:, None] * np.arange(frame)[None, :] % frame
    angles = phases * (2.0 * math.pi / frame)
    full = np.where((part == 0)[:, None], np.cos(angles), -np.sin(angles)) / math.sqrt(frame)
    full = full.astype(np.float32)
    high = full.astype(ml_dtypes.bfloat16)
    low = (full - high.astype(np.float32)).astype(ml_dtypes.bfloat16)
    return high, low


def split(value):
    high = value.astype(jnp.bfloat16)
    return high, (value - high.astype(jnp.float32)).astype(jnp.bfloat16)


def nt_dot(a, b):
    return lax.dot_general(a, b, (((1,), (1,)), ((), ())), preferred_element_type=jnp.float32)


def channelize(volt, taps_ref, high_ref, low_ref, spec, wide, filt, inter):
    taps, frame = taps_ref.shape
    half = frame // 2
    frames = volt.shape[0] // 8
    spectra = frames - taps + 1
    wide[...] = volt[...].astype(jnp.float32)
    row = lax.broadcasted_iota(jnp.int32, (8, half), 0)
    second = (row // 2) % 2 == 1
    pattern = []
    for p in range(taps):
        first_half = jnp.broadcast_to(taps_ref[p : p + 1, :half], (8, half))
        other_half = jnp.broadcast_to(taps_ref[p : p + 1, half:], (8, half))
        pattern.append(jnp.where(second, other_half, first_half)[None])
    block = 128
    for j in range(2):
        for part in range(4 * spectra // block):
            base = j * 4 * frames + part * block
            total = None
            for p in range(taps):
                rows = wide[base + 4 * p : base + 4 * p + block, :].reshape(block // 8, 8, half)
                term = rows * pattern[p]
                total = term if total is None else total + term
            at = (j * 4 * spectra) + part * block
            filt[at : at + block, :] = total.reshape(block, half)
    columns = []
    for b in range(2):
        for j in range(2):
            start = j * 4 * spectra + b
            columns.append(
                jnp.concatenate(
                    [
                        filt[pl.ds(start, spectra, stride=4), :],
                        filt[pl.ds(start + 2, spectra, stride=4), :],
                    ],
                    axis=1,
                )
            )
    frames_high, frames_low = split(jnp.concatenate(columns, axis=0))
    high, low = high_ref[...], low_ref[...]
    result = nt_dot(high, frames_high) + (nt_dot(high, frames_low) + nt_dot(low, frames_high))
    channels = high.shape[0] // 2
    for b in range(2):
        for part in range(2):
            for j in range(2):
                column = (b * 2 + j) * spectra
                inter[b, part, :, j, :] = result[
                    part * channels : (part + 1) * channels, column : column + spectra
                ]
    for b in range(2):
        for part in range(2):
            spec[b * 2 + part] = (
                inter[b, part].astype(jnp.bfloat16).reshape(NZ, NY, NX, 2, spectra)
            )


def spread_kernel(
    parts, volt_hbm, taps_hbm, high_hbm, low_hbm, out,
    volt, taps, high, low, wide, filt, inter, spec, near,
    load_sem, own_sem, z_send, z_recv, plane_send, plane_recv, core_send, core_recv,
):
    loads = [
        pltpu.make_async_copy(source, target, load_sem.at[i])
        for i, (source, target) in enumerate(((volt_hbm, volt), (taps_hbm, taps), (high_hbm, high), (low_hbm, low)))
    ]
    for load in loads:
        load.start()

    chan, pair = lax.axis_index("chan"), lax.axis_index("pair")
    y, z, x_hi = chan // (NZ * NX), (chan // NX) % NZ, chan % NX
    x = x_hi * 2 + pair // 2
    core = pair % 2
    quad, place = z // 4, z % 4
    core_mate = pair + 1 - 2 * core
    x_mate = (pair + 2) % 4

    def z_ahead(r, k):
        return (quad + r) % QUADS * 4 + (place + k) % 4

    def z_behind(r, k):
        return (quad - r + QUADS) % QUADS * 4 + (place - k + 4) % 4

    def along_z(oz):
        return {"chan": (y * NZ + oz) * NX + x_hi, "pair": pair}

    def in_plane(oy, ox):
        return {"chan": (oy * NZ + z) * NX + ox // 2, "pair": ox % 2 * 2 + core}

    barrier = pltpu.get_barrier_semaphore()

    def greet(device):
        pl.semaphore_signal(barrier, inc=1, device_id=device, device_id_type=MESH)

    for r, k in Z_STEPS:
        greet(along_z(z_ahead(r, k)))
    for dy, dx in PLANE_STEPS:
        greet(in_plane((y + dy) % NY, (x + dx) % (2 * NX)))
    greet({"chan": chan, "pair": core_mate})

    for load in loads:
        load.wait()
    channelize(volt, taps, high, low, spec, wide, filt, inter)
    pl.semaphore_wait(barrier, len(Z_STEPS) + len(PLANE_STEPS) + 1)

    def remote(source, target, send, recv, device):
        return pltpu.make_async_remote_copy(
            src_ref=source, dst_ref=target, send_sem=send, recv_sem=recv,
            device_id=device, device_id_type=MESH,
        )

    size = 4 // parts

    def rows(p):
        return pl.ds(p * size, size)

    def z_copy(p, r, k):
        oz = z_ahead(r, k)
        return remote(
            spec.at[rows(p), oz], near.at[rows(p), :, :, z],
            z_send.at[p, r * 4 + k], z_recv.at[p, r * 4 + k], along_z(oz),
        )

    def z_arrival(p, r, k):
        oz = z_behind(r, k)
        return remote(
            spec.at[rows(p), oz], near.at[rows(p), :, :, oz],
            z_send.at[p, r * 4 + k], z_recv.at[p, r * 4 + k], along_z(oz),
        )

    def plane_copy(p, dy, dx):
        oy, ox = (y + dy) % NY, (x + dx) % (2 * NX)
        return remote(
            near.at[rows(p), oy, ox // 2], out.at[rows(p), pair, y, :, x_hi],
            plane_send.at[p, dy * 4 + dx], plane_recv.at[p, dy * 4 + dx], in_plane(oy, ox),
        )

    def plane_arrival(p, dy, dx):
        oy, ox = (y - dy + NY) % NY, (x - dx + 2 * NX) % (2 * NX)
        return remote(
            near.at[rows(p), oy, ox // 2], out.at[rows(p), ox % 2 * 2 + core, oy, :, ox // 2],
            plane_send.at[p, dy * 4 + dx], plane_recv.at[p, dy * 4 + dx], in_plane(oy, ox),
        )

    def core_copy(p, block, odd):
        ref = out.at[rows(p), block]
        return remote(
            ref, ref, core_send.at[p, odd], core_recv.at[p, odd], {"chan": chan, "pair": core_mate}
        )

    own_z = [
        pltpu.make_async_copy(spec.at[rows(p), z], near.at[rows(p), :, :, z], own_sem.at[p]) for p in range(parts)
    ]
    own = [
        pltpu.make_async_copy(near.at[rows(p), y, x_hi], out.at[rows(p), pair, y, :, x_hi], own_sem.at[parts + p])
        for p in range(parts)
    ]

    for p in range(parts):
        for r, k in Z_STEPS:
            z_copy(p, r, k).start()
        own_z[p].start()

    def spread(p):
        own_z[p].wait()
        for r, k in Z_STEPS:
            z_arrival(p, r, k).wait_recv()
        for dy, dx in PLANE_STEPS:
            plane_copy(p, dy, dx).start()
        own[p].start()

    def share(p):
        for odd, block in ((1, x_mate), (0, pair)):
            if not odd:
                own[p].wait()
            for dy, dx in PLANE_STEPS:
                if dx % 2 == odd:
                    plane_arrival(p, dy, dx).wait_recv()
            core_copy(p, block, odd).start()

    spread(0)
    for p in range(1, parts):
        spread(p)
        share(p - 1)
    share(parts - 1)

    for p in range(parts):
        core_copy(p, (x_mate + 1 - 2 * core), 1).wait_recv()
        core_copy(p, core_mate, 0).wait_recv()
        core_copy(p, x_mate, 1).wait_send()
        core_copy(p, pair, 0).wait_send()
        for r, k in Z_STEPS:
            z_copy(p, r, k).wait_send()
        for dy, dx in PLANE_STEPS:
            plane_copy(p, dy, dx).wait_send()


def correlate_kernel(scale, everyone, out, result, out_sem):
    tiles, _, block, tile = result.shape
    mine = pl.ds(pl.multiple_of(lax.axis_index("pair") * block, block), block)
    rows = [everyone[q, mine, :] for q in range(4)]
    straight = jnp.concatenate(rows, axis=1)
    turned = jnp.concatenate([rows[1], -rows[0], rows[3], -rows[2]], axis=1)
    stores = []
    for g in range(tiles):
        there = pl.ds(g * tile, tile)
        columns = jnp.concatenate([everyone[q, there, :] for q in range(4)], axis=1)
        result[g, 0] = nt_dot(straight, columns) * scale
        result[g, 1] = nt_dot(turned, columns) * scale
        stores.append(pltpu.make_async_copy(result.at[g], out.at[0, :, :, there], out_sem.at[g]))
        stores[g].start()
    for store in stores:
        store.wait()


def shards(voltages, fir_taps):
    _, antennas, batches, samples = voltages.shape
    taps, frame = fir_taps.shape
    frames = samples // frame
    spectra_len = frames - taps + 1
    half = frame // 2
    volt = voltages.reshape(antennas, batches, samples // half, half)
    volt = with_layout_constraint(volt, Layout(major_to_minor=(0, 2, 1, 3)))
    volt = jnp.transpose(volt, (0, 2, 1, 3)).reshape(antennas * batches * samples // half, half)
    high, low = dft_matrix(half)
    hbm = pl.BlockSpec(memory_space=pltpu.HBM)
    vmem = pl.BlockSpec(memory_space=pltpu.VMEM)
    dma = pltpu.SemaphoreType.DMA
    everyone = pl.pallas_call(
        functools.partial(spread_kernel, PARTS),
        out_shape=pltpu.VMEM((4, 4, NY, NZ, NX, 2, spectra_len), jnp.bfloat16),
        in_specs=[hbm] * 4,
        out_specs=vmem,
        scratch_shapes=[
            pltpu.VMEM(volt.shape, jnp.bfloat16),
            pltpu.VMEM(fir_taps.shape, jnp.float32),
            pltpu.VMEM(high.shape, jnp.bfloat16),
            pltpu.VMEM(low.shape, jnp.bfloat16),
            pltpu.VMEM(volt.shape, jnp.float32),
            pltpu.VMEM((8 * spectra_len, half), jnp.float32),
            pltpu.VMEM((2, 2, half, 2, spectra_len), jnp.float32),
            pltpu.VMEM((4, NZ, NY, NX, 2, spectra_len), jnp.bfloat16),
            pltpu.VMEM((4, NY, NX, NZ, 2, spectra_len), jnp.bfloat16),
            dma((4,)),
            dma((2 * PARTS,)),
            dma((PARTS, NZ)),
            dma((PARTS, NZ)),
            dma((PARTS, NY * 2 * NX)),
            dma((PARTS, NY * 2 * NX)),
            dma((PARTS, 2)),
            dma((PARTS, 2)),
        ],
        compiler_params=pltpu.CompilerParams(
            collective_id=0, has_side_effects=True, vmem_limit_bytes=VMEM_LIMIT
        ),
    )(volt, fir_taps, jnp.asarray(high), jnp.asarray(low))
    everyone = everyone.reshape(4, 4 * NY * NZ * NX * 2, spectra_len)
    total = everyone.shape[1]
    block = total // 4
    tiles = 4
    tile = total // tiles
    scale = 1.0 / math.sqrt(batches * spectra_len)
    return pl.pallas_call(
        functools.partial(correlate_kernel, scale),
        out_shape=jax.ShapeDtypeStruct((1, 2, block, total), jnp.float32),
        in_specs=[vmem],
        out_specs=hbm,
        scratch_shapes=[pltpu.VMEM((tiles, 2, block, tile), jnp.float32), dma((tiles,))],
        compiler_params=pltpu.CompilerParams(vmem_limit_bytes=8 * 1024 * 1024),
    )(everyone)


def solution(mesh):
    in_specs = (P("pair", "chan", None, None), P())
    out_specs = P("chan", None, "pair", None)
    return jax.shard_map(shards, mesh=mesh, in_specs=in_specs, out_specs=out_specs, check_vma=False)
```

```python
import functools
import math

import jax
import jax.numpy as jnp
import ml_dtypes
import numpy as np
from jax import lax
from jax.experimental import pallas as pl
from jax.experimental.layout import Layout, with_layout_constraint
from jax.experimental.pallas import tpu as pltpu
from jax.sharding import PartitionSpec as P

MESH = pl.DeviceIdType.MESH
NY, NZ, NX = 4, 16, 2
Z_ORDER = (0, 4, 1, 5, 2, 6, 3, 7, 12, 8, 13, 9, 14, 10, 15, 11)
PARTS = 2
PLANE_STEPS = sorted(
    ((dy, dx) for dy in range(NY) for dx in range(2 * NX) if dy or dx),
    key=lambda step: -(min(step[0], NY - step[0]) + min(step[1], 2 * NX - step[1])),
)
VMEM_LIMIT = 56 * 1024 * 1024


def dft_matrix(channels):
    frame = 2 * channels
    part, z, y, x = np.meshgrid(np.arange(2), np.arange(NZ), np.arange(NY), np.arange(NX), indexing="ij")
    freq = ((y * NZ + z) * NX + x).reshape(-1)
    part = part.reshape(-1)
    phases = freq[:, None] * np.arange(frame)[None, :] % frame
    angles = phases * (2.0 * math.pi / frame)
    full = np.where((part == 0)[:, None], np.cos(angles), -np.sin(angles)) / math.sqrt(frame)
    full = full.astype(np.float32)
    high = full.astype(ml_dtypes.bfloat16)
    low = (full - high.astype(np.float32)).astype(ml_dtypes.bfloat16)
    return high, low


def split(value):
    high = value.astype(jnp.bfloat16)
    return high, (value - high.astype(jnp.float32)).astype(jnp.bfloat16)


def nt_dot(a, b):
    return lax.dot_general(a, b, (((1,), (1,)), ((), ())), preferred_element_type=jnp.float32)


def channelize(volt, taps_ref, high_ref, low_ref, spec, wide, filt, inter):
    taps, frame = taps_ref.shape
    half = frame // 2
    frames = volt.shape[0] // 8
    spectra = frames - taps + 1
    wide[...] = volt[...].astype(jnp.float32)
    row = lax.broadcasted_iota(jnp.int32, (8, half), 0)
    second = (row // 2) % 2 == 1
    pattern = []
    for p in range(taps):
        first_half = jnp.broadcast_to(taps_ref[p : p + 1, :half], (8, half))
        other_half = jnp.broadcast_to(taps_ref[p : p + 1, half:], (8, half))
        pattern.append(jnp.where(second, other_half, first_half)[None])
    block = 128
    for j in range(2):
        for part in range(4 * spectra // block):
            base = j * 4 * frames + part * block
            total = None
            for p in range(taps):
                rows = wide[base + 4 * p : base + 4 * p + block, :].reshape(block // 8, 8, half)
                term = rows * pattern[p]
                total = term if total is None else total + term
            at = (j * 4 * spectra) + part * block
            filt[at : at + block, :] = total.reshape(block, half)
    columns = []
    for b in range(2):
        for j in range(2):
            start = j * 4 * spectra + b
            columns.append(
                jnp.concatenate(
                    [
                        filt[pl.ds(start, spectra, stride=4), :],
                        filt[pl.ds(start + 2, spectra, stride=4), :],
                    ],
                    axis=1,
                )
            )
    frames_high, frames_low = split(jnp.concatenate(columns, axis=0))
    high, low = high_ref[...], low_ref[...]
    result = nt_dot(high, frames_high) + (nt_dot(high, frames_low) + nt_dot(low, frames_high))
    channels = high.shape[0] // 2
    for b in range(2):
        for part in range(2):
            for j in range(2):
                column = (b * 2 + j) * spectra
                inter[b, part, :, j, :] = result[
                    part * channels : (part + 1) * channels, column : column + spectra
                ]
    for b in range(2):
        for part in range(2):
            spec[b * 2 + part] = (
                inter[b, part].astype(jnp.bfloat16).reshape(NZ, NY, NX, 2, spectra)
            )


def spread_kernel(
    parts, volt_hbm, taps_hbm, high_hbm, low_hbm, out,
    volt, taps, high, low, wide, filt, inter, spec, near,
    load_sem, own_sem, z_send, z_recv, plane_send, plane_recv, core_send, core_recv,
):
    loads = [
        pltpu.make_async_copy(source, target, load_sem.at[i])
        for i, (source, target) in enumerate(((volt_hbm, volt), (taps_hbm, taps), (high_hbm, high), (low_hbm, low)))
    ]
    for load in loads:
        load.start()

    chan, pair = lax.axis_index("chan"), lax.axis_index("pair")
    y, z, x_hi = chan // (NZ * NX), (chan // NX) % NZ, chan % NX
    x = x_hi * 2 + pair // 2
    core = pair % 2
    core_mate = pair + 1 - 2 * core
    x_mate = (pair + 2) % 4

    def others(steps, each):
        for oz in steps:
            pl.when(z != oz)(functools.partial(each, oz))

    def along_z(oz):
        return {"chan": (y * NZ + oz) * NX + x_hi, "pair": pair}

    def in_plane(oy, ox):
        return {"chan": (oy * NZ + z) * NX + ox // 2, "pair": ox % 2 * 2 + core}

    barrier = pltpu.get_barrier_semaphore()

    def greet(device):
        pl.semaphore_signal(barrier, inc=1, device_id=device, device_id_type=MESH)

    for step in range(1, NZ):
        greet(along_z((z + (NZ // 2 + step // 2 if step % 2 else NZ // 2 - step // 2)) % NZ))
    for dy, dx in PLANE_STEPS:
        greet(in_plane((y + dy) % NY, (x + dx) % (2 * NX)))
    greet({"chan": chan, "pair": core_mate})

    for load in loads:
        load.wait()
    channelize(volt, taps, high, low, spec, wide, filt, inter)
    pl.semaphore_wait(barrier, NZ - 1 + len(PLANE_STEPS) + 1)

    def remote(source, target, send, recv, device):
        return pltpu.make_async_remote_copy(
            src_ref=source, dst_ref=target, send_sem=send, recv_sem=recv,
            device_id=device, device_id_type=MESH,
        )

    size = 4 // parts

    def rows(p):
        return pl.ds(p * size, size)

    def z_copy(p, oz):
        return remote(
            spec.at[rows(p), oz], near.at[rows(p), :, :, z], z_send.at[p, oz], z_recv.at[p, z], along_z(oz)
        )

    def z_arrival(p, oz):
        return remote(
            spec.at[rows(p), oz], near.at[rows(p), :, :, oz], z_send.at[p, oz], z_recv.at[p, oz], along_z(oz)
        )

    def plane_copy(p, dy, dx):
        oy, ox = (y + dy) % NY, (x + dx) % (2 * NX)
        return remote(
            near.at[rows(p), oy, ox // 2], out.at[rows(p), pair, y, :, x_hi],
            plane_send.at[p, dy * 4 + dx], plane_recv.at[p, dy * 4 + dx], in_plane(oy, ox),
        )

    def plane_arrival(p, dy, dx):
        oy, ox = (y - dy + NY) % NY, (x - dx + 2 * NX) % (2 * NX)
        return remote(
            near.at[rows(p), oy, ox // 2], out.at[rows(p), ox % 2 * 2 + core, oy, :, ox // 2],
            plane_send.at[p, dy * 4 + dx], plane_recv.at[p, dy * 4 + dx], in_plane(oy, ox),
        )

    def core_copy(p, block, odd):
        ref = out.at[rows(p), block]
        return remote(
            ref, ref, core_send.at[p, odd], core_recv.at[p, odd], {"chan": chan, "pair": core_mate}
        )

    own_z = [
        pltpu.make_async_copy(spec.at[rows(p), z], near.at[rows(p), :, :, z], own_sem.at[p]) for p in range(parts)
    ]
    own = [
        pltpu.make_async_copy(near.at[rows(p), y, x_hi], out.at[rows(p), pair, y, :, x_hi], own_sem.at[parts + p])
        for p in range(parts)
    ]

    def send(oz):
        for p in range(parts):
            z_copy(p, oz).start()

    for p in range(parts):
        own_z[p].start()
    others(Z_ORDER, send)

    def spread(p):
        own_z[p].wait()
        others(range(NZ), lambda oz: z_arrival(p, oz).wait_recv())
        for dy, dx in PLANE_STEPS:
            plane_copy(p, dy, dx).start()
        own[p].start()

    def share(p):
        for odd, block in ((1, x_mate), (0, pair)):
            if not odd:
                own[p].wait()
            for dy, dx in PLANE_STEPS:
                if dx % 2 == odd:
                    plane_arrival(p, dy, dx).wait_recv()
            core_copy(p, block, odd).start()

    spread(0)
    for p in range(1, parts):
        spread(p)
        share(p - 1)
    share(parts - 1)

    for p in range(parts):
        core_copy(p, (x_mate + 1 - 2 * core), 1).wait_recv()
        core_copy(p, core_mate, 0).wait_recv()
        core_copy(p, x_mate, 1).wait_send()
        core_copy(p, pair, 0).wait_send()
        others(range(NZ), lambda oz: z_copy(p, oz).wait_send())
        for dy, dx in PLANE_STEPS:
            plane_copy(p, dy, dx).wait_send()


def correlate_kernel(scale, everyone, out, result, out_sem):
    tiles, _, block, tile = result.shape
    mine = pl.ds(pl.multiple_of(lax.axis_index("pair") * block, block), block)
    rows = [everyone[q, mine, :] for q in range(4)]
    straight = jnp.concatenate(rows, axis=1)
    turned = jnp.concatenate([rows[1], -rows[0], rows[3], -rows[2]], axis=1)
    stores = []
    for g in range(tiles):
        there = pl.ds(g * tile, tile)
        columns = jnp.concatenate([everyone[q, there, :] for q in range(4)], axis=1)
        result[g, 0] = nt_dot(straight, columns) * scale
        result[g, 1] = nt_dot(turned, columns) * scale
        stores.append(pltpu.make_async_copy(result.at[g], out.at[0, :, :, there], out_sem.at[g]))
        stores[g].start()
    for store in stores:
        store.wait()


def shards(voltages, fir_taps):
    _, antennas, batches, samples = voltages.shape
    taps, frame = fir_taps.shape
    frames = samples // frame
    spectra_len = frames - taps + 1
    half = frame // 2
    volt = voltages.reshape(antennas, batches, samples // half, half)
    volt = with_layout_constraint(volt, Layout(major_to_minor=(0, 2, 1, 3)))
    volt = jnp.transpose(volt, (0, 2, 1, 3)).reshape(antennas * batches * samples // half, half)
    high, low = dft_matrix(half)
    hbm = pl.BlockSpec(memory_space=pltpu.HBM)
    vmem = pl.BlockSpec(memory_space=pltpu.VMEM)
    dma = pltpu.SemaphoreType.DMA
    everyone = pl.pallas_call(
        functools.partial(spread_kernel, PARTS),
        out_shape=pltpu.VMEM((4, 4, NY, NZ, NX, 2, spectra_len), jnp.bfloat16),
        in_specs=[hbm] * 4,
        out_specs=vmem,
        scratch_shapes=[
            pltpu.VMEM(volt.shape, jnp.bfloat16),
            pltpu.VMEM(fir_taps.shape, jnp.float32),
            pltpu.VMEM(high.shape, jnp.bfloat16),
            pltpu.VMEM(low.shape, jnp.bfloat16),
            pltpu.VMEM(volt.shape, jnp.float32),
            pltpu.VMEM((8 * spectra_len, half), jnp.float32),
            pltpu.VMEM((2, 2, half, 2, spectra_len), jnp.float32),
            pltpu.VMEM((4, NZ, NY, NX, 2, spectra_len), jnp.bfloat16),
            pltpu.VMEM((4, NY, NX, NZ, 2, spectra_len), jnp.bfloat16),
            dma((4,)),
            dma((2 * PARTS,)),
            dma((PARTS, NZ)),
            dma((PARTS, NZ)),
            dma((PARTS, NY * 2 * NX)),
            dma((PARTS, NY * 2 * NX)),
            dma((PARTS, 2)),
            dma((PARTS, 2)),
        ],
        compiler_params=pltpu.CompilerParams(
            collective_id=0, has_side_effects=True, vmem_limit_bytes=VMEM_LIMIT
        ),
    )(volt, fir_taps, jnp.asarray(high), jnp.asarray(low))
    everyone = everyone.reshape(4, 4 * NY * NZ * NX * 2, spectra_len)
    total = everyone.shape[1]
    block = total // 4
    tiles = 4
    tile = total // tiles
    scale = 1.0 / math.sqrt(batches * spectra_len)
    return pl.pallas_call(
        functools.partial(correlate_kernel, scale),
        out_shape=jax.ShapeDtypeStruct((1, 2, block, total), jnp.float32),
        in_specs=[vmem],
        out_specs=hbm,
        scratch_shapes=[pltpu.VMEM((tiles, 2, block, tile), jnp.float32), dma((tiles,))],
        compiler_params=pltpu.CompilerParams(vmem_limit_bytes=8 * 1024 * 1024),
    )(everyone)


def solution(mesh):
    in_specs = (P("pair", "chan", None, None), P())
    out_specs = P("chan", None, "pair", None)
    return jax.shard_map(shards, mesh=mesh, in_specs=in_specs, out_specs=out_specs, check_vma=False)
```

```python
import functools
import math

import jax
import jax.numpy as jnp
import ml_dtypes
import numpy as np
from jax import lax
from jax.experimental import pallas as pl
from jax.experimental.layout import Layout, with_layout_constraint
from jax.experimental.pallas import tpu as pltpu
from jax.sharding import PartitionSpec as P

MESH = pl.DeviceIdType.MESH
NY, NZ, NX = 4, 16, 2
STARTS = (0.0, 0.7, 1.6, 2.5, 4.1, 5.0, 5.9, 6.9, 8.4, 8.4, 8.4, 8.4, 7.8, 7.8, 7.8, 7.8)
DUE, FAR = 1.0, 0.65
EARLY = 7
RELAY = {oz: EARLY - 1 if oz < (EARLY + NZ + 1) // 2 else 0 for oz in range(EARLY, NZ)}


def hops(a, b):
    return min((a - b) % NZ, (b - a) % NZ)


Z_TABLE = [
    sorted(
        (o for o in range(NZ) if o != z),
        key=lambda o: (z >= EARLY and o >= EARLY, DUE * STARTS[o] - FAR * hops(z, o), (o - z) % NZ),
    )
    for z in range(NZ)
]
PARTS = 2
PLANE_STEPS = sorted(
    ((dy, dx) for dy in range(NY) for dx in range(2 * NX) if dy or dx),
    key=lambda step: -(min(step[0], NY - step[0]) + min(step[1], 2 * NX - step[1])),
)
VMEM_LIMIT = 56 * 1024 * 1024


def dft_matrix(channels):
    frame = 2 * channels
    part, z, y, x = np.meshgrid(np.arange(2), np.arange(NZ), np.arange(NY), np.arange(NX), indexing="ij")
    freq = ((y * NZ + z) * NX + x).reshape(-1)
    part = part.reshape(-1)
    phases = freq[:, None] * np.arange(frame)[None, :] % frame
    angles = phases * (2.0 * math.pi / frame)
    full = np.where((part == 0)[:, None], np.cos(angles), -np.sin(angles)) / math.sqrt(frame)
    full = full.astype(np.float32)
    high = full.astype(ml_dtypes.bfloat16)
    low = (full - high.astype(np.float32)).astype(ml_dtypes.bfloat16)
    return high, low


def split(value):
    high = value.astype(jnp.bfloat16)
    return high, (value - high.astype(jnp.float32)).astype(jnp.bfloat16)


def nt_dot(a, b):
    return lax.dot_general(a, b, (((1,), (1,)), ((), ())), preferred_element_type=jnp.float32)


def channelize(volt, taps_ref, high_ref, low_ref, spec, wide, filt, inter):
    taps, frame = taps_ref.shape
    half = frame // 2
    frames = volt.shape[0] // 8
    spectra = frames - taps + 1
    wide[...] = volt[...].astype(jnp.float32)
    row = lax.broadcasted_iota(jnp.int32, (8, half), 0)
    second = (row // 2) % 2 == 1
    pattern = []
    for p in range(taps):
        first_half = jnp.broadcast_to(taps_ref[p : p + 1, :half], (8, half))
        other_half = jnp.broadcast_to(taps_ref[p : p + 1, half:], (8, half))
        pattern.append(jnp.where(second, other_half, first_half)[None])
    block = 128
    for j in range(2):
        for part in range(4 * spectra // block):
            base = j * 4 * frames + part * block
            total = None
            for p in range(taps):
                rows = wide[base + 4 * p : base + 4 * p + block, :].reshape(block // 8, 8, half)
                term = rows * pattern[p]
                total = term if total is None else total + term
            at = (j * 4 * spectra) + part * block
            filt[at : at + block, :] = total.reshape(block, half)
    columns = []
    for b in range(2):
        for j in range(2):
            start = j * 4 * spectra + b
            columns.append(
                jnp.concatenate(
                    [
                        filt[pl.ds(start, spectra, stride=4), :],
                        filt[pl.ds(start + 2, spectra, stride=4), :],
                    ],
                    axis=1,
                )
            )
    frames_high, frames_low = split(jnp.concatenate(columns, axis=0))
    high, low = high_ref[...], low_ref[...]
    result = nt_dot(high, frames_high) + (nt_dot(high, frames_low) + nt_dot(low, frames_high))
    channels = high.shape[0] // 2
    for b in range(2):
        for part in range(2):
            for j in range(2):
                column = (b * 2 + j) * spectra
                inter[b, part, :, j, :] = result[
                    part * channels : (part + 1) * channels, column : column + spectra
                ]
    for b in range(2):
        for part in range(2):
            spec[b * 2 + part] = (
                inter[b, part].astype(jnp.bfloat16).reshape(NZ, NY, NX, 2, spectra)
            )


def spread_kernel(
    parts, volt_hbm, taps_hbm, high_hbm, low_hbm, out,
    volt, taps, high, low, wide, filt, inter, spec, near,
    late_sem, load_sem, own_sem, z_send, z_recv, plane_send, plane_recv, core_send, core_recv,
):
    loads = [
        pltpu.make_async_copy(source, target, load_sem.at[i])
        for i, (source, target) in enumerate(((volt_hbm, volt), (taps_hbm, taps), (high_hbm, high), (low_hbm, low)))
    ]
    for load in loads:
        load.start()

    chan, pair = lax.axis_index("chan"), lax.axis_index("pair")
    y, z, x_hi = chan // (NZ * NX), (chan // NX) % NZ, chan % NX
    x = x_hi * 2 + pair // 2
    core = pair % 2
    core_mate = pair + 1 - 2 * core
    x_mate = (pair + 2) % 4

    def others(steps, each):
        for oz in steps:
            pl.when(z != oz)(functools.partial(each, oz))

    def along_z(oz):
        return {"chan": (y * NZ + oz) * NX + x_hi, "pair": pair}

    def in_plane(oy, ox):
        return {"chan": (oy * NZ + z) * NX + ox // 2, "pair": ox % 2 * 2 + core}

    barrier = pltpu.get_barrier_semaphore()

    def greet(device):
        pl.semaphore_signal(barrier, inc=1, device_id=device, device_id_type=MESH)

    for step in range(1, NZ):
        oz = (z + (NZ // 2 + step // 2 if step % 2 else NZ // 2 - step // 2)) % NZ
        pl.when(jnp.logical_or(z < EARLY, oz < EARLY))(functools.partial(greet, along_z(oz)))
    for dy, dx in PLANE_STEPS:
        greet(in_plane((y + dy) % NY, (x + dx) % (2 * NX)))
    greet({"chan": chan, "pair": core_mate})

    for load in loads:
        load.wait()
    channelize(volt, taps, high, low, spec, wide, filt, inter)
    mates = len(PLANE_STEPS) + 1

    @pl.when(z >= EARLY)
    def _():
        pl.semaphore_wait(barrier, EARLY + mates)

    @pl.when(z < EARLY)
    def _():
        pl.semaphore_wait(barrier, NZ - 1 + mates)

    for relay in sorted(set(RELAY.values())):

        @pl.when(z == relay)
        def _():
            for oz in RELAY:
                if RELAY[oz] == relay:
                    pl.semaphore_signal(late_sem, inc=1, device_id=along_z(oz), device_id_type=MESH)

    def remote(source, target, send, recv, device):
        return pltpu.make_async_remote_copy(
            src_ref=source, dst_ref=target, send_sem=send, recv_sem=recv,
            device_id=device, device_id_type=MESH,
        )

    size = 4 // parts

    def rows(p):
        return pl.ds(p * size, size)

    def z_copy(p, oz):
        return remote(
            spec.at[rows(p), oz], near.at[rows(p), :, :, z], z_send.at[p, oz], z_recv.at[p, z], along_z(oz)
        )

    def z_arrival(p, oz):
        return remote(
            spec.at[rows(p), oz], near.at[rows(p), :, :, oz], z_send.at[p, oz], z_recv.at[p, oz], along_z(oz)
        )

    def plane_copy(p, dy, dx):
        oy, ox = (y + dy) % NY, (x + dx) % (2 * NX)
        return remote(
            near.at[rows(p), oy, ox // 2], out.at[rows(p), pair, y, :, x_hi],
            plane_send.at[p, dy * 4 + dx], plane_recv.at[p, dy * 4 + dx], in_plane(oy, ox),
        )

    def plane_arrival(p, dy, dx):
        oy, ox = (y - dy + NY) % NY, (x - dx + 2 * NX) % (2 * NX)
        return remote(
            near.at[rows(p), oy, ox // 2], out.at[rows(p), ox % 2 * 2 + core, oy, :, ox // 2],
            plane_send.at[p, dy * 4 + dx], plane_recv.at[p, dy * 4 + dx], in_plane(oy, ox),
        )

    def core_copy(p, block, odd):
        ref = out.at[rows(p), block]
        return remote(
            ref, ref, core_send.at[p, odd], core_recv.at[p, odd], {"chan": chan, "pair": core_mate}
        )

    own_z = [
        pltpu.make_async_copy(spec.at[rows(p), z], near.at[rows(p), :, :, z], own_sem.at[p]) for p in range(parts)
    ]
    own = [
        pltpu.make_async_copy(near.at[rows(p), y, x_hi], out.at[rows(p), pair, y, :, x_hi], own_sem.at[parts + p])
        for p in range(parts)
    ]

    def send(oz):
        for p in range(parts):
            z_copy(p, oz).start()

    for p in range(parts):
        own_z[p].start()
    for step in range(NZ - 1):
        if step == EARLY:

            @pl.when(z >= EARLY)
            def _():
                pl.semaphore_wait(late_sem, 1)

        target = Z_TABLE[0][step]
        for oz in range(1, NZ):
            target = jnp.where(z == oz, Z_TABLE[oz][step], target)
        send(target)

    def spread(p):
        own_z[p].wait()
        others(range(NZ), lambda oz: z_arrival(p, oz).wait_recv())
        for dy, dx in PLANE_STEPS:
            plane_copy(p, dy, dx).start()
        own[p].start()

    def share(p):
        for odd, block in ((1, x_mate), (0, pair)):
            if not odd:
                own[p].wait()
            for dy, dx in PLANE_STEPS:
                if dx % 2 == odd:
                    plane_arrival(p, dy, dx).wait_recv()
            core_copy(p, block, odd).start()

    spread(0)
    for p in range(1, parts):
        spread(p)
        share(p - 1)
    share(parts - 1)

    for p in range(parts):
        core_copy(p, (x_mate + 1 - 2 * core), 1).wait_recv()
        core_copy(p, core_mate, 0).wait_recv()
        core_copy(p, x_mate, 1).wait_send()
        core_copy(p, pair, 0).wait_send()
        others(range(NZ), lambda oz: z_copy(p, oz).wait_send())
        for dy, dx in PLANE_STEPS:
            plane_copy(p, dy, dx).wait_send()


def correlate_kernel(scale, everyone, out, result, out_sem):
    tiles, _, block, tile = result.shape
    mine = pl.ds(pl.multiple_of(lax.axis_index("pair") * block, block), block)
    rows = [everyone[q, mine, :] for q in range(4)]
    straight = jnp.concatenate(rows, axis=1)
    turned = jnp.concatenate([rows[1], -rows[0], rows[3], -rows[2]], axis=1)
    stores = []
    for g in range(tiles):
        there = pl.ds(g * tile, tile)
        columns = jnp.concatenate([everyone[q, there, :] for q in range(4)], axis=1)
        result[g, 0] = nt_dot(straight, columns) * scale
        result[g, 1] = nt_dot(turned, columns) * scale
        stores.append(pltpu.make_async_copy(result.at[g], out.at[0, :, :, there], out_sem.at[g]))
        stores[g].start()
    for store in stores:
        store.wait()


def shards(voltages, fir_taps):
    _, antennas, batches, samples = voltages.shape
    taps, frame = fir_taps.shape
    frames = samples // frame
    spectra_len = frames - taps + 1
    half = frame // 2
    volt = voltages.reshape(antennas, batches, samples // half, half)
    volt = with_layout_constraint(volt, Layout(major_to_minor=(0, 2, 1, 3)))
    volt = jnp.transpose(volt, (0, 2, 1, 3)).reshape(antennas * batches * samples // half, half)
    high, low = dft_matrix(half)
    hbm = pl.BlockSpec(memory_space=pltpu.HBM)
    vmem = pl.BlockSpec(memory_space=pltpu.VMEM)
    dma = pltpu.SemaphoreType.DMA
    everyone = pl.pallas_call(
        functools.partial(spread_kernel, PARTS),
        out_shape=pltpu.VMEM((4, 4, NY, NZ, NX, 2, spectra_len), jnp.bfloat16),
        in_specs=[hbm] * 4,
        out_specs=vmem,
        scratch_shapes=[
            pltpu.VMEM(volt.shape, jnp.bfloat16),
            pltpu.VMEM(fir_taps.shape, jnp.float32),
            pltpu.VMEM(high.shape, jnp.bfloat16),
            pltpu.VMEM(low.shape, jnp.bfloat16),
            pltpu.VMEM(volt.shape, jnp.float32),
            pltpu.VMEM((8 * spectra_len, half), jnp.float32),
            pltpu.VMEM((2, 2, half, 2, spectra_len), jnp.float32),
            pltpu.VMEM((4, NZ, NY, NX, 2, spectra_len), jnp.bfloat16),
            pltpu.VMEM((4, NY, NX, NZ, 2, spectra_len), jnp.bfloat16),
            pltpu.SemaphoreType.REGULAR,
            dma((4,)),
            dma((2 * PARTS,)),
            dma((PARTS, NZ)),
            dma((PARTS, NZ)),
            dma((PARTS, NY * 2 * NX)),
            dma((PARTS, NY * 2 * NX)),
            dma((PARTS, 2)),
            dma((PARTS, 2)),
        ],
        compiler_params=pltpu.CompilerParams(
            collective_id=0, has_side_effects=True, vmem_limit_bytes=VMEM_LIMIT
        ),
    )(volt, fir_taps, jnp.asarray(high), jnp.asarray(low))
    everyone = everyone.reshape(4, 4 * NY * NZ * NX * 2, spectra_len)
    total = everyone.shape[1]
    block = total // 4
    tiles = 4
    tile = total // tiles
    scale = 1.0 / math.sqrt(batches * spectra_len)
    return pl.pallas_call(
        functools.partial(correlate_kernel, scale),
        out_shape=jax.ShapeDtypeStruct((1, 2, block, total), jnp.float32),
        in_specs=[vmem],
        out_specs=hbm,
        scratch_shapes=[pltpu.VMEM((tiles, 2, block, tile), jnp.float32), dma((tiles,))],
        compiler_params=pltpu.CompilerParams(vmem_limit_bytes=8 * 1024 * 1024),
    )(everyone)


def solution(mesh):
    in_specs = (P("pair", "chan", None, None), P())
    out_specs = P("chan", None, "pair", None)
    return jax.shard_map(shards, mesh=mesh, in_specs=in_specs, out_specs=out_specs, check_vma=False)
```

```python
import functools
import math

import jax
import jax.numpy as jnp
import ml_dtypes
import numpy as np
from jax import lax
from jax.experimental import pallas as pl
from jax.experimental.layout import Layout, with_layout_constraint
from jax.experimental.pallas import tpu as pltpu
from jax.sharding import PartitionSpec as P

MESH = pl.DeviceIdType.MESH
NY, NZ, NX = 4, 16, 2
STARTS = (0.0, 0.7, 1.6, 2.5, 4.1, 5.0, 5.9, 6.9, 8.4, 8.4, 8.4, 8.4, 7.8, 7.8, 7.8, 7.8)
DUE, FAR = 1.0, 0.65
EARLY = 6
CORE_ORDER = (2, 1, 3, 0)
RELAY = {oz: EARLY - 1 if oz < (EARLY + NZ + 1) // 2 else 0 for oz in range(EARLY, NZ)}


def hops(a, b):
    return min((a - b) % NZ, (b - a) % NZ)


Z_TABLE = [
    sorted(
        (o for o in range(NZ) if o != z),
        key=lambda o: (z >= EARLY and o >= EARLY, DUE * STARTS[o] - FAR * hops(z, o), (o - z) % NZ),
    )
    for z in range(NZ)
]
PARTS = 1
PLANE_STEPS = sorted(
    ((dy, dx) for dy in range(NY) for dx in range(2 * NX) if dy or dx),
    key=lambda step: -(min(step[0], NY - step[0]) + min(step[1], 2 * NX - step[1])),
)
VMEM_LIMIT = 56 * 1024 * 1024


def dft_matrix(channels):
    frame = 2 * channels
    part, z, y, x = np.meshgrid(np.arange(2), np.arange(NZ), np.arange(NY), np.arange(NX), indexing="ij")
    freq = ((y * NZ + z) * NX + x).reshape(-1)
    part = part.reshape(-1)
    phases = freq[:, None] * np.arange(frame)[None, :] % frame
    angles = phases * (2.0 * math.pi / frame)
    full = np.where((part == 0)[:, None], np.cos(angles), -np.sin(angles)) / math.sqrt(frame)
    full = full.astype(np.float32)
    high = full.astype(ml_dtypes.bfloat16)
    low = (full - high.astype(np.float32)).astype(ml_dtypes.bfloat16)
    return high, low


def split(value):
    high = value.astype(jnp.bfloat16)
    return high, (value - high.astype(jnp.float32)).astype(jnp.bfloat16)


def nt_dot(a, b):
    return lax.dot_general(a, b, (((1,), (1,)), ((), ())), preferred_element_type=jnp.float32)


def channelize(volt, taps_ref, high_ref, low_ref, spec, wide, filt, inter):
    taps, frame = taps_ref.shape
    half = frame // 2
    frames = volt.shape[0] // 8
    spectra = frames - taps + 1
    wide[...] = volt[...].astype(jnp.float32)
    row = lax.broadcasted_iota(jnp.int32, (8, half), 0)
    second = (row // 2) % 2 == 1
    pattern = []
    for p in range(taps):
        first_half = jnp.broadcast_to(taps_ref[p : p + 1, :half], (8, half))
        other_half = jnp.broadcast_to(taps_ref[p : p + 1, half:], (8, half))
        pattern.append(jnp.where(second, other_half, first_half)[None])
    block = 128
    for j in range(2):
        for part in range(4 * spectra // block):
            base = j * 4 * frames + part * block
            total = None
            for p in range(taps):
                rows = wide[base + 4 * p : base + 4 * p + block, :].reshape(block // 8, 8, half)
                term = rows * pattern[p]
                total = term if total is None else total + term
            at = (j * 4 * spectra) + part * block
            filt[at : at + block, :] = total.reshape(block, half)
    columns = []
    for b in range(2):
        for j in range(2):
            start = j * 4 * spectra + b
            columns.append(
                jnp.concatenate(
                    [
                        filt[pl.ds(start, spectra, stride=4), :],
                        filt[pl.ds(start + 2, spectra, stride=4), :],
                    ],
                    axis=1,
                )
            )
    frames_high, frames_low = split(jnp.concatenate(columns, axis=0))
    high, low = high_ref[...], low_ref[...]
    result = nt_dot(high, frames_high) + (nt_dot(high, frames_low) + nt_dot(low, frames_high))
    channels = high.shape[0] // 2
    for b in range(2):
        for part in range(2):
            for j in range(2):
                column = (b * 2 + j) * spectra
                inter[b, part, :, j, :] = result[
                    part * channels : (part + 1) * channels, column : column + spectra
                ]
    for b in range(2):
        for part in range(2):
            spec[b * 2 + part] = (
                inter[b, part].astype(jnp.bfloat16).reshape(NZ, NY, NX, 2, spectra)
            )


def spread_kernel(
    parts, volt_hbm, taps_hbm, high_hbm, low_hbm, out,
    volt, taps, high, low, wide, filt, inter, spec, near,
    late_sem, load_sem, own_sem, z_send, z_recv, plane_send, plane_recv, core_send, core_recv,
):
    loads = [
        pltpu.make_async_copy(source, target, load_sem.at[i])
        for i, (source, target) in enumerate(((volt_hbm, volt), (taps_hbm, taps), (high_hbm, high), (low_hbm, low)))
    ]
    for load in loads:
        load.start()

    chan, pair = lax.axis_index("chan"), lax.axis_index("pair")
    y, z, x_hi = chan // (NZ * NX), (chan // NX) % NZ, chan % NX
    x = x_hi * 2 + pair // 2
    core = pair % 2
    core_mate = pair + 1 - 2 * core
    x_mate = (pair + 2) % 4

    def others(steps, each):
        for oz in steps:
            pl.when(z != oz)(functools.partial(each, oz))

    def along_z(oz):
        return {"chan": (y * NZ + oz) * NX + x_hi, "pair": pair}

    def in_plane(oy, ox):
        return {"chan": (oy * NZ + z) * NX + ox // 2, "pair": ox % 2 * 2 + core}

    barrier = pltpu.get_barrier_semaphore()

    def greet(device):
        pl.semaphore_signal(barrier, inc=1, device_id=device, device_id_type=MESH)

    for step in range(1, NZ):
        oz = (z + (NZ // 2 + step // 2 if step % 2 else NZ // 2 - step // 2)) % NZ
        pl.when(jnp.logical_or(z < EARLY, oz < EARLY))(functools.partial(greet, along_z(oz)))
    for dy, dx in PLANE_STEPS:
        greet(in_plane((y + dy) % NY, (x + dx) % (2 * NX)))
    greet({"chan": chan, "pair": core_mate})

    for load in loads:
        load.wait()
    channelize(volt, taps, high, low, spec, wide, filt, inter)
    mates = len(PLANE_STEPS) + 1

    @pl.when(z >= EARLY)
    def _():
        pl.semaphore_wait(barrier, EARLY + mates)

    @pl.when(z < EARLY)
    def _():
        pl.semaphore_wait(barrier, NZ - 1 + mates)

    for relay in sorted(set(RELAY.values())):

        @pl.when(z == relay)
        def _():
            for oz in RELAY:
                if RELAY[oz] == relay:
                    pl.semaphore_signal(late_sem, inc=1, device_id=along_z(oz), device_id_type=MESH)

    def remote(source, target, send, recv, device):
        return pltpu.make_async_remote_copy(
            src_ref=source, dst_ref=target, send_sem=send, recv_sem=recv,
            device_id=device, device_id_type=MESH,
        )

    size = 4 // parts

    def rows(p):
        return pl.ds(p * size, size)

    def z_copy(p, oz):
        return remote(
            spec.at[rows(p), oz], near.at[rows(p), :, :, z], z_send.at[p, oz], z_recv.at[p, z], along_z(oz)
        )

    def z_arrival(p, oz):
        return remote(
            spec.at[rows(p), oz], near.at[rows(p), :, :, oz], z_send.at[p, oz], z_recv.at[p, oz], along_z(oz)
        )

    def plane_copy(p, dy, dx):
        oy, ox = (y + dy) % NY, (x + dx) % (2 * NX)
        return remote(
            near.at[rows(p), oy, ox // 2], out.at[rows(p), pair, y, :, x_hi],
            plane_send.at[p, dy * 4 + dx], plane_recv.at[p, dy * 4 + dx], in_plane(oy, ox),
        )

    def plane_arrival(p, dy, dx):
        oy, ox = (y - dy + NY) % NY, (x - dx + 2 * NX) % (2 * NX)
        return remote(
            near.at[rows(p), oy, ox // 2], out.at[rows(p), ox % 2 * 2 + core, oy, :, ox // 2],
            plane_send.at[p, dy * 4 + dx], plane_recv.at[p, dy * 4 + dx], in_plane(oy, ox),
        )

    def core_copy(p, block, odd, dy):
        ref = out.at[rows(p), block, (y - dy + NY) % NY]
        at = odd * NY + dy
        return remote(
            ref, ref, core_send.at[p, at], core_recv.at[p, at], {"chan": chan, "pair": core_mate}
        )

    own_z = [
        pltpu.make_async_copy(spec.at[rows(p), z], near.at[rows(p), :, :, z], own_sem.at[p]) for p in range(parts)
    ]
    own = [
        pltpu.make_async_copy(near.at[rows(p), y, x_hi], out.at[rows(p), pair, y, :, x_hi], own_sem.at[parts + p])
        for p in range(parts)
    ]

    for p in range(parts):
        own_z[p].start()
    def target(step):
        oz = Z_TABLE[0][step]
        for own_plane in range(1, NZ):
            oz = jnp.where(z == own_plane, Z_TABLE[own_plane][step], oz)
        return oz

    early_steps = [target(step) for step in range(EARLY)]
    late_steps = [target(step) for step in range(EARLY, NZ - 1)]
    for p in range(parts):
        for oz in early_steps:
            z_copy(p, oz).start()

    @pl.when(z >= EARLY)
    def _():
        pl.semaphore_wait(late_sem, 1)

    for p in range(parts):
        for oz in late_steps:
            z_copy(p, oz).start()

    def spread(p):
        own_z[p].wait()
        others(range(NZ), lambda oz: z_arrival(p, oz).wait_recv())
        for dy, dx in PLANE_STEPS:
            plane_copy(p, dy, dx).start()
        own[p].start()

    def share(p):
        for dy in CORE_ORDER:
            for odd, block in ((0, pair), (1, x_mate)):
                if not odd and not dy:
                    own[p].wait()
                for step in PLANE_STEPS:
                    if step[0] == dy and step[1] % 2 == odd:
                        plane_arrival(p, *step).wait_recv()
                core_copy(p, block, odd, dy).start()

    spread(0)
    for p in range(1, parts):
        spread(p)
        share(p - 1)
    share(parts - 1)

    for p in range(parts):
        for dy in range(NY):
            core_copy(p, x_mate + 1 - 2 * core, 1, dy).wait_recv()
            core_copy(p, core_mate, 0, dy).wait_recv()
            core_copy(p, x_mate, 1, dy).wait_send()
            core_copy(p, pair, 0, dy).wait_send()
        others(range(NZ), lambda oz: z_copy(p, oz).wait_send())
        for dy, dx in PLANE_STEPS:
            plane_copy(p, dy, dx).wait_send()


def correlate_kernel(scale, everyone, out, result, out_sem):
    tiles, _, block, tile = result.shape
    mine = pl.ds(pl.multiple_of(lax.axis_index("pair") * block, block), block)
    rows = [everyone[q, mine, :] for q in range(4)]
    straight = jnp.concatenate(rows, axis=1)
    turned = jnp.concatenate([rows[1], -rows[0], rows[3], -rows[2]], axis=1)
    stores = []
    for g in range(tiles):
        there = pl.ds(g * tile, tile)
        columns = jnp.concatenate([everyone[q, there, :] for q in range(4)], axis=1)
        result[g, 0] = nt_dot(straight, columns) * scale
        result[g, 1] = nt_dot(turned, columns) * scale
        stores.append(pltpu.make_async_copy(result.at[g], out.at[0, :, :, there], out_sem.at[g]))
        stores[g].start()
    for store in stores:
        store.wait()


def shards(voltages, fir_taps):
    _, antennas, batches, samples = voltages.shape
    taps, frame = fir_taps.shape
    frames = samples // frame
    spectra_len = frames - taps + 1
    half = frame // 2
    volt = voltages.reshape(antennas, batches, samples // half, half)
    volt = with_layout_constraint(volt, Layout(major_to_minor=(0, 2, 1, 3)))
    volt = jnp.transpose(volt, (0, 2, 1, 3)).reshape(antennas * batches * samples // half, half)
    high, low = dft_matrix(half)
    hbm = pl.BlockSpec(memory_space=pltpu.HBM)
    vmem = pl.BlockSpec(memory_space=pltpu.VMEM)
    dma = pltpu.SemaphoreType.DMA
    everyone = pl.pallas_call(
        functools.partial(spread_kernel, PARTS),
        out_shape=pltpu.VMEM((4, 4, NY, NZ, NX, 2, spectra_len), jnp.bfloat16),
        in_specs=[hbm] * 4,
        out_specs=vmem,
        scratch_shapes=[
            pltpu.VMEM(volt.shape, jnp.bfloat16),
            pltpu.VMEM(fir_taps.shape, jnp.float32),
            pltpu.VMEM(high.shape, jnp.bfloat16),
            pltpu.VMEM(low.shape, jnp.bfloat16),
            pltpu.VMEM(volt.shape, jnp.float32),
            pltpu.VMEM((8 * spectra_len, half), jnp.float32),
            pltpu.VMEM((2, 2, half, 2, spectra_len), jnp.float32),
            pltpu.VMEM((4, NZ, NY, NX, 2, spectra_len), jnp.bfloat16),
            pltpu.VMEM((4, NY, NX, NZ, 2, spectra_len), jnp.bfloat16),
            pltpu.SemaphoreType.REGULAR,
            dma((4,)),
            dma((2 * PARTS,)),
            dma((PARTS, NZ)),
            dma((PARTS, NZ)),
            dma((PARTS, NY * 2 * NX)),
            dma((PARTS, NY * 2 * NX)),
            dma((PARTS, 2 * NY)),
            dma((PARTS, 2 * NY)),
        ],
        compiler_params=pltpu.CompilerParams(
            collective_id=0, has_side_effects=True, vmem_limit_bytes=VMEM_LIMIT
        ),
    )(volt, fir_taps, jnp.asarray(high), jnp.asarray(low))
    everyone = everyone.reshape(4, 4 * NY * NZ * NX * 2, spectra_len)
    total = everyone.shape[1]
    block = total // 4
    tiles = 4
    tile = total // tiles
    scale = 1.0 / math.sqrt(batches * spectra_len)
    return pl.pallas_call(
        functools.partial(correlate_kernel, scale),
        out_shape=jax.ShapeDtypeStruct((1, 2, block, total), jnp.float32),
        in_specs=[vmem],
        out_specs=hbm,
        scratch_shapes=[pltpu.VMEM((tiles, 2, block, tile), jnp.float32), dma((tiles,))],
        compiler_params=pltpu.CompilerParams(vmem_limit_bytes=8 * 1024 * 1024),
    )(everyone)


def solution(mesh):
    in_specs = (P("pair", "chan", None, None), P())
    out_specs = P("chan", None, "pair", None)
    return jax.shard_map(shards, mesh=mesh, in_specs=in_specs, out_specs=out_specs, check_vma=False)
```

```python
import functools
import math

import jax
import jax.numpy as jnp
import ml_dtypes
import numpy as np
from jax import lax
from jax.experimental import pallas as pl
from jax.experimental.layout import Layout, with_layout_constraint
from jax.experimental.pallas import tpu as pltpu
from jax.sharding import PartitionSpec as P

MESH = pl.DeviceIdType.MESH
NY, NZ, NX = 4, 16, 2
STARTS = (0.0, 0.7, 1.6, 2.5, 4.1, 5.0, 5.9, 6.9, 8.4, 8.4, 8.4, 8.4, 7.8, 7.8, 7.8, 7.8)
DUE, FAR = 1.0, 0.65
EARLY = 6
CORE_ORDER = (2, 1, 3, 0)
RELAY = {oz: EARLY - 1 if oz < (EARLY + NZ + 1) // 2 else 0 for oz in range(EARLY, NZ)}


def hops(a, b):
    return min((a - b) % NZ, (b - a) % NZ)


Z_TABLE = [
    sorted(
        (o for o in range(NZ) if o != z),
        key=lambda o: (z >= EARLY and o >= EARLY, DUE * STARTS[o] - FAR * hops(z, o), (o - z) % NZ),
    )
    for z in range(NZ)
]
PARTS = 1
PLANE_STEPS = sorted(
    ((dy, dx) for dy in range(NY) for dx in range(2 * NX) if dy or dx),
    key=lambda step: -(min(step[0], NY - step[0]) + min(step[1], 2 * NX - step[1])),
)
VMEM_LIMIT = 56 * 1024 * 1024


def dft_matrix(channels):
    frame = 2 * channels
    part, z, y, x = np.meshgrid(np.arange(2), np.arange(NZ), np.arange(NY), np.arange(NX), indexing="ij")
    freq = ((y * NZ + z) * NX + x).reshape(-1)
    part = part.reshape(-1)
    phases = freq[:, None] * np.arange(frame)[None, :] % frame
    angles = phases * (2.0 * math.pi / frame)
    full = np.where((part == 0)[:, None], np.cos(angles), -np.sin(angles)) / math.sqrt(frame)
    full = full.astype(np.float32)
    high = full.astype(ml_dtypes.bfloat16)
    low = (full - high.astype(np.float32)).astype(ml_dtypes.bfloat16)
    return high, low


def split(value):
    high = value.astype(jnp.bfloat16)
    return high, (value - high.astype(jnp.float32)).astype(jnp.bfloat16)


def nt_dot(a, b):
    return lax.dot_general(a, b, (((1,), (1,)), ((), ())), preferred_element_type=jnp.float32)


def channelize(volt, taps_ref, high_ref, low_ref, spec, wide, filt, inter):
    taps, frame = taps_ref.shape
    half = frame // 2
    frames = volt.shape[0] // 8
    spectra = frames - taps + 1
    wide[...] = volt[...].astype(jnp.float32)
    row = lax.broadcasted_iota(jnp.int32, (8, half), 0)
    second = (row // 2) % 2 == 1
    pattern = []
    for p in range(taps):
        first_half = jnp.broadcast_to(taps_ref[p : p + 1, :half], (8, half))
        other_half = jnp.broadcast_to(taps_ref[p : p + 1, half:], (8, half))
        pattern.append(jnp.where(second, other_half, first_half)[None])
    block = 128
    for j in range(2):
        for part in range(4 * spectra // block):
            base = j * 4 * frames + part * block
            total = None
            for p in range(taps):
                rows = wide[base + 4 * p : base + 4 * p + block, :].reshape(block // 8, 8, half)
                term = rows * pattern[p]
                total = term if total is None else total + term
            at = (j * 4 * spectra) + part * block
            filt[at : at + block, :] = total.reshape(block, half)
    columns = []
    for b in range(2):
        for j in range(2):
            start = j * 4 * spectra + b
            columns.append(
                jnp.concatenate(
                    [
                        filt[pl.ds(start, spectra, stride=4), :],
                        filt[pl.ds(start + 2, spectra, stride=4), :],
                    ],
                    axis=1,
                )
            )
    frames_high, frames_low = split(jnp.concatenate(columns, axis=0))
    high, low = high_ref[...], low_ref[...]
    result = nt_dot(high, frames_high) + (nt_dot(high, frames_low) + nt_dot(low, frames_high))
    channels = high.shape[0] // 2
    for b in range(2):
        for part in range(2):
            for j in range(2):
                column = (b * 2 + j) * spectra
                inter[b, part, :, j, :] = result[
                    part * channels : (part + 1) * channels, column : column + spectra
                ]
    for b in range(2):
        for part in range(2):
            spec[b * 2 + part] = (
                inter[b, part].astype(jnp.bfloat16).reshape(NZ, NY, NX, 2, spectra)
            )


def spread_kernel(
    parts, volt_hbm, taps_hbm, high_hbm, low_hbm, out,
    volt, taps, high, low, wide, filt, inter, spec, near,
    late_sem, load_sem, own_sem, z_send, z_recv, plane_send, plane_recv, core_send, core_recv,
):
    loads = [
        pltpu.make_async_copy(source, target, load_sem.at[i])
        for i, (source, target) in enumerate(((volt_hbm, volt), (taps_hbm, taps), (high_hbm, high), (low_hbm, low)))
    ]
    for load in loads:
        load.start()

    chan, pair = lax.axis_index("chan"), lax.axis_index("pair")
    y, z, x_hi = chan // (NZ * NX), (chan // NX) % NZ, chan % NX
    x = x_hi * 2 + pair // 2
    core = pair % 2
    core_mate = pair + 1 - 2 * core
    x_mate = (pair + 2) % 4

    def others(steps, each):
        for oz in steps:
            pl.when(z != oz)(functools.partial(each, oz))

    def along_z(oz):
        return {"chan": (y * NZ + oz) * NX + x_hi, "pair": pair}

    def in_plane(oy, ox):
        return {"chan": (oy * NZ + z) * NX + ox // 2, "pair": ox % 2 * 2 + core}

    barrier = pltpu.get_barrier_semaphore()

    def greet(device):
        pl.semaphore_signal(barrier, inc=1, device_id=device, device_id_type=MESH)

    for step in range(1, NZ):
        oz = (z + (NZ // 2 + step // 2 if step % 2 else NZ // 2 - step // 2)) % NZ
        pl.when(jnp.logical_or(z < EARLY, oz < EARLY))(functools.partial(greet, along_z(oz)))
    for dy, dx in PLANE_STEPS:
        greet(in_plane((y + dy) % NY, (x + dx) % (2 * NX)))
    greet({"chan": chan, "pair": core_mate})

    for load in loads:
        load.wait()
    channelize(volt, taps, high, low, spec, wide, filt, inter)
    mates = len(PLANE_STEPS) + 1

    @pl.when(z >= EARLY)
    def _():
        pl.semaphore_wait(barrier, EARLY + mates)

    @pl.when(z < EARLY)
    def _():
        pl.semaphore_wait(barrier, NZ - 1 + mates)

    for relay in sorted(set(RELAY.values())):

        @pl.when(z == relay)
        def _():
            for oz in RELAY:
                if RELAY[oz] == relay:
                    pl.semaphore_signal(late_sem, inc=1, device_id=along_z(oz), device_id_type=MESH)

    def remote(source, target, send, recv, device):
        return pltpu.make_async_remote_copy(
            src_ref=source, dst_ref=target, send_sem=send, recv_sem=recv,
            device_id=device, device_id_type=MESH,
        )

    size = 4 // parts

    def rows(p):
        return pl.ds(p * size, size)

    def z_copy(p, oz):
        return remote(
            spec.at[rows(p), oz], near.at[rows(p), :, :, z], z_send.at[p, oz], z_recv.at[p, z], along_z(oz)
        )

    def z_arrival(p, oz):
        return remote(
            spec.at[rows(p), oz], near.at[rows(p), :, :, oz], z_send.at[p, oz], z_recv.at[p, oz], along_z(oz)
        )

    def plane_copy(p, dy, dx):
        oy, ox = (y + dy) % NY, (x + dx) % (2 * NX)
        return remote(
            near.at[rows(p), oy, ox // 2], out.at[rows(p), pair, y, :, x_hi],
            plane_send.at[p, dy * 4 + dx], plane_recv.at[p, dy * 4 + dx], in_plane(oy, ox),
        )

    def plane_arrival(p, dy, dx):
        oy, ox = (y - dy + NY) % NY, (x - dx + 2 * NX) % (2 * NX)
        return remote(
            near.at[rows(p), oy, ox // 2], out.at[rows(p), ox % 2 * 2 + core, oy, :, ox // 2],
            plane_send.at[p, dy * 4 + dx], plane_recv.at[p, dy * 4 + dx], in_plane(oy, ox),
        )

    def core_copy(p, block, odd, dy):
        ref = out.at[rows(p), block, (y - dy + NY) % NY]
        at = odd * NY + dy
        return remote(
            ref, ref, core_send.at[p, at], core_recv.at[p, at], {"chan": chan, "pair": core_mate}
        )

    own_z = [
        pltpu.make_async_copy(spec.at[rows(p), z], near.at[rows(p), :, :, z], own_sem.at[p]) for p in range(parts)
    ]
    own = [
        pltpu.make_async_copy(near.at[rows(p), y, x_hi], out.at[rows(p), pair, y, :, x_hi], own_sem.at[parts + p])
        for p in range(parts)
    ]

    for p in range(parts):
        own_z[p].start()
    def target(step):
        oz = Z_TABLE[0][step]
        for own_plane in range(1, NZ):
            oz = jnp.where(z == own_plane, Z_TABLE[own_plane][step], oz)
        return oz

    early_steps = [target(step) for step in range(EARLY)]
    late_steps = [target(step) for step in range(EARLY, NZ - 1)]
    for p in range(parts):
        for oz in early_steps:
            z_copy(p, oz).start()

    @pl.when(z >= EARLY)
    def _():
        pl.semaphore_wait(late_sem, 1)

    for p in range(parts):
        for oz in late_steps:
            z_copy(p, oz).start()

    def spread(p):
        own_z[p].wait()
        others(range(NZ), lambda oz: z_arrival(p, oz).wait_recv())
        for dy, dx in PLANE_STEPS:
            plane_copy(p, dy, dx).start()
        own[p].start()

    def share(p):
        for dy in CORE_ORDER:
            for odd, block in ((0, pair), (1, x_mate)):
                if not odd and not dy:
                    own[p].wait()
                for step in PLANE_STEPS:
                    if step[0] == dy and step[1] % 2 == odd:
                        plane_arrival(p, *step).wait_recv()
                core_copy(p, block, odd, dy).start()

    spread(0)
    for p in range(1, parts):
        spread(p)
        share(p - 1)
    share(parts - 1)

    for p in range(parts):
        for dy in range(NY):
            core_copy(p, x_mate + 1 - 2 * core, 1, dy).wait_recv()
            core_copy(p, core_mate, 0, dy).wait_recv()
            core_copy(p, x_mate, 1, dy).wait_send()
            core_copy(p, pair, 0, dy).wait_send()
        others(range(NZ), lambda oz: z_copy(p, oz).wait_send())
        for dy, dx in PLANE_STEPS:
            plane_copy(p, dy, dx).wait_send()


def correlate_kernel(scale, everyone, out, result, out_sem):
    tiles, _, block, tile = result.shape
    mine = pl.ds(pl.multiple_of(lax.axis_index("pair") * block, block), block)
    rows = [everyone[q, mine, :] for q in range(4)]
    straight = jnp.concatenate(rows, axis=1)
    turned = jnp.concatenate([rows[1], -rows[0], rows[3], -rows[2]], axis=1)
    stores = []
    for g in range(tiles):
        there = pl.ds(g * tile, tile)
        columns = jnp.concatenate([everyone[q, there, :] for q in range(4)], axis=1)
        for part, side in enumerate((straight, turned)):
            result[g, part] = nt_dot(side, columns) * scale
            store = pltpu.make_async_copy(result.at[g, part], out.at[0, part, :, there], out_sem.at[g, part])
            store.start()
            stores.append(store)
    for store in stores:
        store.wait()


def shards(voltages, fir_taps):
    _, antennas, batches, samples = voltages.shape
    taps, frame = fir_taps.shape
    frames = samples // frame
    spectra_len = frames - taps + 1
    half = frame // 2
    volt = voltages.reshape(antennas, batches, samples // half, half)
    volt = with_layout_constraint(volt, Layout(major_to_minor=(0, 2, 1, 3)))
    volt = jnp.transpose(volt, (0, 2, 1, 3)).reshape(antennas * batches * samples // half, half)
    high, low = dft_matrix(half)
    hbm = pl.BlockSpec(memory_space=pltpu.HBM)
    vmem = pl.BlockSpec(memory_space=pltpu.VMEM)
    dma = pltpu.SemaphoreType.DMA
    everyone = pl.pallas_call(
        functools.partial(spread_kernel, PARTS),
        out_shape=pltpu.VMEM((4, 4, NY, NZ, NX, 2, spectra_len), jnp.bfloat16),
        in_specs=[hbm] * 4,
        out_specs=vmem,
        scratch_shapes=[
            pltpu.VMEM(volt.shape, jnp.bfloat16),
            pltpu.VMEM(fir_taps.shape, jnp.float32),
            pltpu.VMEM(high.shape, jnp.bfloat16),
            pltpu.VMEM(low.shape, jnp.bfloat16),
            pltpu.VMEM(volt.shape, jnp.float32),
            pltpu.VMEM((8 * spectra_len, half), jnp.float32),
            pltpu.VMEM((2, 2, half, 2, spectra_len), jnp.float32),
            pltpu.VMEM((4, NZ, NY, NX, 2, spectra_len), jnp.bfloat16),
            pltpu.VMEM((4, NY, NX, NZ, 2, spectra_len), jnp.bfloat16),
            pltpu.SemaphoreType.REGULAR,
            dma((4,)),
            dma((2 * PARTS,)),
            dma((PARTS, NZ)),
            dma((PARTS, NZ)),
            dma((PARTS, NY * 2 * NX)),
            dma((PARTS, NY * 2 * NX)),
            dma((PARTS, 2 * NY)),
            dma((PARTS, 2 * NY)),
        ],
        compiler_params=pltpu.CompilerParams(
            collective_id=0, has_side_effects=True, vmem_limit_bytes=VMEM_LIMIT
        ),
    )(volt, fir_taps, jnp.asarray(high), jnp.asarray(low))
    everyone = everyone.reshape(4, 4 * NY * NZ * NX * 2, spectra_len)
    total = everyone.shape[1]
    block = total // 4
    tiles = 4
    tile = total // tiles
    scale = 1.0 / math.sqrt(batches * spectra_len)
    return pl.pallas_call(
        functools.partial(correlate_kernel, scale),
        out_shape=jax.ShapeDtypeStruct((1, 2, block, total), jnp.float32),
        in_specs=[vmem],
        out_specs=hbm,
        scratch_shapes=[pltpu.VMEM((tiles, 2, block, tile), jnp.float32), dma((tiles, 2))],
        compiler_params=pltpu.CompilerParams(vmem_limit_bytes=8 * 1024 * 1024),
    )(everyone)


def solution(mesh):
    in_specs = (P("pair", "chan", None, None), P())
    out_specs = P("chan", None, "pair", None)
    return jax.shard_map(shards, mesh=mesh, in_specs=in_specs, out_specs=out_specs, check_vma=False)
```
